512 devices in a mesh: facet: 16 (over z), sub: 8 (over x, core), vis: 4 (over y).
Axes of the slice: x: 4, y: 4, z: 16, core: 2. Of those that a mesh axis runs over, the one named last changes fastest.
Arguments:
- facet_data: bfloat16 [2, 16, 256, 2048], P(None, 'facet', 'vis', 'sub'), may hold values from -6 to 6
- facet_taper: float32 [16, 256], replicated, may hold values from 0.5 to 2
- subgrid_offsets: int32 [16, 8], replicated, may hold values from 0 to 65535
- kernels: bfloat16 [16, 8, 4, 64, 64, 128], P('facet', 'sub', 'vis'), may hold values from -0.75 to 0.75
- block_row: int32 [16, 8, 4, 64], P('facet', 'sub', 'vis'), may hold values from 0 to 63, as said below
- block_col: int32 [16, 8, 4, 64], P('facet', 'sub', 'vis'), may hold values from 0 to 248
- block_count: int32 [16, 8, 4], P('facet', 'sub', 'vis'), may hold values from 8 to 64, as said below
Outputs:
- subgrids: float32 [16, 8, 256, 512], P('facet', 'sub', 'vis')
- visibilities: float32 [16, 8, 4, 64, 256], P('facet', 'sub', 'vis')
The draws below stay inside these ranges and needn't reach their ends.
Inputs may be any that keep to these rules, and one draw needn't show every extreme that they name: `block_row`: A block's 8 rows may reach into the next owner's rows but never past the subgrid's last row. `block_count`: blocks at or past the count are ignored. Some owner is full in every draw.
All inputs are finite; a program needn't handle non-finite values.
Results may differ from the reference program's by a relative error of at most 0.0023.
Values may be sent and summed in bfloat16 or wider, within the bound.
No kernel may reach another device: no remote copies, remote signals or barrier semaphores. Data moves between devices by JAX's collectives and lax.ppermute only.
A program may use at most 64 MiB of HBM per device.

```python
import math
import jax
import jax.numpy as jnp
from jax import lax

N_IMAGE = 65536
YB = 2048
XC = 256
KS = 8
NV = 128
BLK = 64
FACETS = 16
N_FACET = 16
N_SUB = 8
N_VIS = 4


def draw_block_row(key, part):
    key = jax.random.fold_in(key, 11)
    grid_shape = (N_FACET, N_SUB, N_VIS, BLK)
    owner = lax.broadcasted_iota(jnp.int32, grid_shape, 2)
    upper = jnp.where(owner == N_VIS - 1, XC // N_VIS - KS + 1, XC // N_VIS)
    return jax.random.randint(key, grid_shape, 0, upper, dtype=jnp.int32)


def draw_block_count(key, part):
    key = jax.random.fold_in(key, 23)
    first_key, second_key = jax.random.split(key)
    grid_shape = (N_FACET, N_SUB, N_VIS)
    counts = jax.random.randint(first_key, grid_shape, max(BLK // 8, 1), BLK + 1, dtype=jnp.int32)
    chosen = jax.random.randint(second_key, (), 0, N_FACET * N_SUB * N_VIS, dtype=jnp.int32)
    filled = jnp.arange(N_FACET * N_SUB * N_VIS, dtype=jnp.int32).reshape(grid_shape) == chosen
    return jnp.where(filled, BLK, counts)


def plant(drawn, own_key, low, largest):
    extent = drawn.shape
    spot = [jax.random.randint(jax.random.fold_in(own_key, axis), (), 0, extent[axis]) for axis in range(len(extent))]
    drawn = drawn.at[tuple(spot)].set(low)
    longest = extent.index(max(extent))
    spot[longest] = (spot[longest] + 1) % extent[longest]
    return drawn.at[tuple(spot)].set(largest)


def block_levels(own_key, dims, pieces, least, high):
    level = 1.0
    for axis_at, shards_of in pieces:
        steps = jax.random.uniform(jax.random.fold_in(jax.random.fold_in(own_key, 6), axis_at), (shards_of,), jnp.float32, least / len(pieces), high / len(pieces))
        level = level * jnp.repeat(jnp.exp(steps), dims[axis_at] // shards_of).reshape((-1,) + (1,) * (len(dims) - 1 - axis_at))
    return level


def bell_draw(own_key, shape, spread, limit, cuts=(), kind=jnp.bfloat16):
    values = spread * jax.random.normal(own_key, shape, jnp.float32)
    if cuts:
        values = values * block_levels(own_key, shape, cuts, -0.22, 0.18)
    return jnp.clip(values, -limit, limit).astype(kind)


def setup_inputs(seed: int = 0) -> dict:
    seeds = jax.random.split(jax.random.key(seed), 8)
    return {
        "facet_data": bell_draw(seeds[0], (2, FACETS, XC, YB), 1.0, 6.0, ((1, 16), (2, 4), (3, 8))),
        "facet_taper": jnp.clip(jnp.exp(jax.random.uniform(seeds[1], (FACETS, XC), jnp.float32, math.log(0.5), math.log(2.0))), 0.5, 2.0),
        "subgrid_offsets": plant(jax.random.randint(seeds[2], (N_FACET, N_SUB), 0, N_IMAGE), jax.random.fold_in(seeds[2], 1), 0, N_IMAGE - 1).astype(jnp.int32),
        "kernels": bell_draw(seeds[3], (N_FACET, N_SUB, N_VIS, BLK, KS * KS, NV), (KS * KS) ** -0.5, 0.75, ((0, 16), (1, 8), (2, 4))),
        "block_row": draw_block_row(jax.random.fold_in(seeds[7], 71), 0),
        "block_col": plant(jax.random.randint(seeds[5], (N_FACET, N_SUB, N_VIS, BLK), 0, XC - KS + 1), jax.random.fold_in(seeds[5], 1), 0, XC - KS).astype(jnp.int32),
        "block_count": draw_block_count(jax.random.fold_in(seeds[7], 71), 0),
    }


def mulmod(multiplier, multiplicand):
    high = multiplier // 256 * multiplicand % 256 * 256
    return (high + multiplier % 256 * multiplicand) % N_IMAGE

def subgrid_freqs(offsets, columns):
    steps = jnp.arange(columns, dtype=jnp.int32)
    return (offsets[:, None] + steps[None, :] - columns // 2) % N_IMAGE

def table_of(samples, frequency):
    turns = mulmod(samples[:, None], frequency[None, :])
    angles = turns.astype(jnp.float32) * (2.0 * math.pi / N_IMAGE)
    return jnp.concatenate([jnp.cos(angles), -jnp.sin(angles)], axis=1).astype(jnp.bfloat16)

def rotate(real_part, imag_part, phase_turns, weight):
    angles = phase_turns.astype(jnp.float32) * (-2.0 * math.pi / N_IMAGE)
    cosine = jnp.cos(angles)
    sine = jnp.sin(angles)
    return jnp.concatenate([weight * (real_part * cosine - imag_part * sine), weight * (real_part * sine + imag_part * cosine)], axis=-1)

def degrid(subgrid, kernel, row_starts, col_starts, live_count, columns):

    def patch(row_first, col_first):
        real_patch = lax.dynamic_slice(subgrid, (row_first.astype(jnp.int32), col_first.astype(jnp.int32)), (KS, KS))
        imag_patch = lax.dynamic_slice(subgrid, (row_first.astype(jnp.int32), (col_first + columns).astype(jnp.int32)), (KS, KS))
        return (real_patch.reshape(-1), imag_patch.reshape(-1))
    real_rows, imag_rows = jax.vmap(patch)(row_starts, col_starts)
    weights = kernel.astype(jnp.float32)
    visibility_real = jnp.einsum('bk,bkn->bn', real_rows, weights, precision=lax.Precision.HIGHEST)
    visibility_imag = jnp.einsum('bk,bkn->bn', imag_rows, weights, precision=lax.Precision.HIGHEST)
    active = (jnp.arange(kernel.shape[0], dtype=jnp.int32) < live_count)[:, None]
    return jnp.where(active, jnp.concatenate([visibility_real, visibility_imag], axis=1), 0.0)

def reference(facet_data, facet_taper, subgrid_offsets, kernels, block_row, block_col, block_count):
    facets = facet_data.shape[1]
    stacked = jnp.transpose(facet_data, (1, 0, 2, 3)).reshape(facets * 2 * XC, YB)
    samples = jnp.arange(YB, dtype=jnp.int32)
    shifts = jnp.arange(facets, dtype=jnp.int32) * YB % N_IMAGE
    weight = facet_taper[:, None, :] * (1.0 / math.sqrt(YB * facets))

    def one_subgrid(offset):
        frequency = subgrid_freqs(offset[None], XC)[0]
        table_rows = table_of(samples, frequency)
        product = jnp.dot(stacked, table_rows, preferred_element_type=jnp.float32).reshape(facets, 2, XC, 2 * XC)
        real_part = product[:, 0, :, :XC] - product[:, 1, :, XC:]
        imag_part = product[:, 0, :, XC:] + product[:, 1, :, :XC]
        phase_turns = mulmod(shifts[:, None], frequency[None, :])[:, None, :]
        return lax.optimization_barrier(jnp.sum(rotate(real_part, imag_part, phase_turns, weight), axis=0))
    subgrids = lax.map(one_subgrid, subgrid_offsets.reshape(-1)).reshape(N_FACET, N_SUB, XC, 2 * XC)
    starts = jnp.arange(N_VIS, dtype=jnp.int32) * (XC // N_VIS)

    def per_subgrid(operands):
        subgrid, kernel, row_first, col_first, live_count = operands

        def per_owner(kernel_one, rows_one, cols_one, count_one):
            return degrid(subgrid, kernel_one, rows_one, cols_one, count_one, XC)
        return jax.vmap(per_owner)(kernel, row_first + starts[:, None], col_first, live_count)
    flat_count = N_FACET * N_SUB
    visibilities = lax.map(per_subgrid, (subgrids.reshape(flat_count, XC, 2 * XC), kernels.reshape((flat_count,) + kernels.shape[2:]), block_row.reshape(flat_count, N_VIS, -1), block_col.reshape(flat_count, N_VIS, -1), block_count.reshape(flat_count, N_VIS)))
    return (subgrids, visibilities.reshape(N_FACET, N_SUB, N_VIS, block_row.shape[3], 2 * kernels.shape[5]))
```

```python
import math

import jax
import jax.numpy as jnp
import numpy as np
from jax import lax
from jax.experimental import pallas as pl
from jax.experimental.pallas import tpu as pltpu
from jax.sharding import PartitionSpec as P

N_IMAGE = 65536
YB = 2048
KS = 8
FINE = 32
COARSE = YB // FINE
WINDOW = 2


def turn_table(left, right):
    turns = (left.astype(np.int64)[:, None] * right.astype(np.int64)[None, :]) % N_IMAGE
    angles = turns * (2.0 * math.pi / N_IMAGE)
    return np.stack([np.cos(angles), -np.sin(angles)]).astype(np.float32)


def predict_kernel(steps_ref, coarse_ref, fine_ref, factor_ref, own_ref, near_ref, out_ref, rows_ref, table_ref):
    columns = coarse_ref.shape[2]
    row_count = own_ref.shape[1]
    pair = out_ref.shape[0]
    for slot in range(pair):
        target = pl.program_id(0) * pair + slot
        real_step = pltpu.roll(steps_ref[0], 128 - target, 1)[:, 0:1]
        imag_step = pltpu.roll(steps_ref[1], 128 - target, 1)[:, 0:1]
        far_real, far_imag = real_step[:COARSE], imag_step[:COARSE]
        low_real, low_imag = real_step[COARSE:], imag_step[COARSE:]
        rows_ref[slot, 0] = far_real * coarse_ref[0] - far_imag * coarse_ref[1]
        rows_ref[slot, 1] = far_real * coarse_ref[1] + far_imag * coarse_ref[0]
        fine_real = low_real * fine_ref[0] - low_imag * fine_ref[1]
        fine_imag = low_real * fine_ref[1] + low_imag * fine_ref[0]
        for a in range(COARSE):
            row_real = rows_ref[slot, 0, pl.ds(a, 1), :]
            row_imag = rows_ref[slot, 1, pl.ds(a, 1), :]
            table_ref[slot, pl.ds(a * FINE, FINE), :columns] = (
                row_real * fine_real - row_imag * fine_imag
            ).astype(jnp.bfloat16)
            table_ref[slot, pl.ds(a * FINE, FINE), columns:] = (
                row_real * fine_imag + row_imag * fine_real
            ).astype(jnp.bfloat16)
    for slot in range(pair):
        total_real = jnp.zeros((row_count, columns), jnp.float32)
        total_imag = jnp.zeros((row_count, columns), jnp.float32)
        for number, ref in enumerate((own_ref, near_ref)):
            samples = ref[...].reshape(2 * row_count, YB)
            product = jnp.dot(samples, table_ref[slot], preferred_element_type=jnp.float32)
            real_part = product[:row_count, :columns] - product[row_count:, columns:]
            imag_part = product[:row_count, columns:] + product[row_count:, :columns]
            cosine = factor_ref[slot, 2 * number : 2 * number + 1, :]
            sine = factor_ref[slot, 2 * number + 1 : 2 * number + 2, :]
            total_real += real_part * cosine - imag_part * sine
            total_imag += real_part * sine + imag_part * cosine
        out_ref[slot, :, :columns] = total_real.astype(jnp.bfloat16)
        out_ref[slot, :, columns:] = total_imag.astype(jnp.bfloat16)


def predict(steps, factors, own, near, columns, targets):
    row_count = own.shape[1]
    pair = 2
    coarse = turn_table(np.arange(COARSE) * FINE, np.arange(columns))
    fine = turn_table(np.arange(FINE), np.arange(columns))
    whole = pl.BlockSpec(memory_space=pltpu.VMEM)
    return pl.pallas_call(
        predict_kernel,
        grid=(targets // pair,),
        out_shape=jax.ShapeDtypeStruct((targets, row_count, 2 * columns), jnp.bfloat16),
        in_specs=[
            whole,
            whole,
            whole,
            pl.BlockSpec((pair, factors.shape[1], columns), lambda i: (i, 0, 0)),
            whole,
            whole,
        ],
        out_specs=pl.BlockSpec((pair, row_count, 2 * columns), lambda i: (i, 0, 0)),
        scratch_shapes=[
            pltpu.VMEM((pair, 2, COARSE, columns), jnp.float32),
            pltpu.VMEM((pair, YB, 2 * columns), jnp.bfloat16),
        ],
        compiler_params=pltpu.CompilerParams(vmem_limit_bytes=32 * 1024 * 1024),
    )(steps, coarse, fine, factors, own, near)


def degrid_kernel(row_ref, col_ref, count_ref, own_ref, rim_ref, kernel_ref, out_ref, extended_ref, flipped_ref):
    columns = own_ref.shape[1] // 2
    row_count = own_ref.shape[0]
    extended_ref[:row_count] = own_ref[...]
    extended_ref[row_count : row_count + KS] = rim_ref[...]
    extended_ref[row_count + KS :] = jnp.zeros_like(extended_ref[row_count + KS :])
    flipped_ref[...] = extended_ref[...].T

    def group(g, carry):
        values = ([], [])
        for j in range(8):
            b = g * 8 + j
            first = row_ref[b]
            start = col_ref[b]
            live = b < count_ref[0]
            weights = kernel_ref[b].astype(jnp.float32)
            shift = lax.rem(128 - first, 128)
            for part in range(2):
                patch = flipped_ref[pl.ds(part * columns + start, KS), :]
                patch = pltpu.roll(patch, shift, 1)
                total = patch[:, 0:1] * weights[:KS]
                for a in range(1, KS):
                    total += patch[:, a : a + 1] * weights[a * KS : (a + 1) * KS]
                value = jnp.sum(total, axis=0, keepdims=True)
                values[part].append(jnp.where(live, value, 0.0))
        for part in range(2):
            out_ref[pl.ds(pl.multiple_of(g * 8, 8), 8), part * 128 : (part + 1) * 128] = (
                jnp.concatenate(values[part], axis=0)
            )
        return carry

    lax.fori_loop(0, kernel_ref.shape[0] // 8, group, 0)


def degrid(own, rim, kernel, row_starts, col_starts, live_count):
    whole = pl.BlockSpec(memory_space=pltpu.VMEM)
    scalar = pl.BlockSpec(memory_space=pltpu.SMEM)
    return pl.pallas_call(
        degrid_kernel,
        out_shape=jax.ShapeDtypeStruct((kernel.shape[0], 2 * kernel.shape[2]), jnp.float32),
        in_specs=[scalar, scalar, scalar, whole, whole, whole],
        out_specs=whole,
        scratch_shapes=[
            pltpu.VMEM((128, own.shape[1]), jnp.float32),
            pltpu.VMEM((own.shape[1], 128), jnp.float32),
        ],
        compiler_params=pltpu.CompilerParams(vmem_limit_bytes=32 * 1024 * 1024),
    )(row_starts, col_starts, live_count, own, rim, kernel)


def cos_sin(turns, sign):
    angles = turns.astype(jnp.float32) * (2.0 * math.pi / N_IMAGE)
    return jnp.cos(angles), sign * jnp.sin(angles)


def on_device(facet_data, facet_taper, subgrid_offsets, kernels, block_row, block_col, block_count):
    facet_index = lax.axis_index("facet")
    sub_index = lax.axis_index("sub")
    facets = lax.axis_size("facet")
    subs = lax.axis_size("sub")
    vis_count = lax.axis_size("vis")
    columns = facet_taper.shape[1]
    row_count = facet_data.shape[2]
    targets = facets // WINDOW
    scale = 1.0 / math.sqrt(YB * facets)
    portion = lax.all_gather(facet_data[:, 0], "sub", axis=2, tiled=True)
    pairs = []
    for z in range(facets):
        for s in range(subs):
            source = (z + 1) % facets if s % 2 == 0 else (z - 1) % facets
            pairs.append((source * subs + s, z * subs + s))
    near = lax.ppermute(portion, ("facet", "sub"), pairs)
    near_index = (facet_index + jnp.where(sub_index % 2 == 0, 1, facets - 1)) % facets

    chosen = facet_index % WINDOW + WINDOW * jnp.arange(targets, dtype=jnp.int32)
    offsets = lax.dynamic_slice_in_dim(subgrid_offsets, sub_index, 1, 1)[:, 0]
    origin = (offsets[chosen] - columns // 2) % N_IMAGE
    multiples = jnp.concatenate(
        [jnp.arange(COARSE, dtype=jnp.int32) * FINE, jnp.arange(FINE, dtype=jnp.int32)]
    )
    step_turns = (multiples[:, None] * origin[None, :]) % N_IMAGE
    step_turns = jnp.pad(step_turns, ((0, 0), (0, 128 - targets)))
    steps = jnp.stack(cos_sin(step_turns, -1.0))
    frequencies = (origin[:, None] + jnp.arange(columns, dtype=jnp.int32)[None, :]) % N_IMAGE
    window = jnp.stack([facet_index, near_index])
    phase_turns = (window[None, :, None] * (YB % N_IMAGE) % N_IMAGE * (frequencies[:, None, :] % 32)) % N_IMAGE
    cosine, sine = cos_sin(phase_turns, -1.0)
    weight = facet_taper[window] * scale
    factors = jnp.stack([weight[None] * cosine, weight[None] * sine], axis=2)
    factors = factors.reshape(targets, 2 * WINDOW, columns)

    partial = predict(steps, factors, portion, near, columns, targets)
    groups = [[r + WINDOW * j for j in range(targets)] for r in range(WINDOW)]
    received = lax.all_to_all(partial, "facet", 0, 0, axis_index_groups=groups, tiled=True)
    summed = jnp.sum(received.astype(jnp.float32), axis=0)
    rim = lax.ppermute(summed[:KS], "vis", [(i, i - 1) for i in range(1, vis_count)])
    visibilities = degrid(
        summed, rim, kernels[0, 0, 0], block_row[0, 0, 0], block_col[0, 0, 0], block_count[0, 0]
    )
    return (
        summed.reshape(1, 1, row_count, 2 * columns),
        visibilities.reshape((1, 1, 1) + visibilities.shape),
    )


def solution(mesh):
    return jax.shard_map(
        on_device,
        mesh=mesh,
        in_specs=(
            P(None, "facet", "vis", "sub"),
            P(),
            P(),
            P("facet", "sub", "vis", None, None, None),
            P("facet", "sub", "vis", None),
            P("facet", "sub", "vis", None),
            P("facet", "sub", "vis"),
        ),
        out_specs=(P("facet", "sub", "vis", None), P("facet", "sub", "vis", None, None)),
        check_vma=False,
    )
```

```python
import math

import jax
import jax.numpy as jnp
import numpy as np
from jax import lax
from jax.experimental import pallas as pl
from jax.experimental.pallas import tpu as pltpu
from jax.sharding import PartitionSpec as P

N_IMAGE = 65536
YB = 2048
KS = 8
FINE = 32
SPREAD = 4


def turn_table(left, right):
    turns = (left.astype(np.int64)[:, None] * right.astype(np.int64)[None, :]) % N_IMAGE
    angles = turns * (2.0 * math.pi / N_IMAGE)
    return np.stack([np.cos(angles), -np.sin(angles)]).astype(np.float32)


def predict_kernel(place_ref, steps_ref, coarse_ref, fine_ref, factor_ref, own_ref, mate_ref, out_ref, rows_ref, table_ref):
    columns = coarse_ref.shape[2]
    window, _, row_count, width = own_ref.shape
    pair = out_ref.shape[0]
    coarse_rows = 2 * width // FINE
    first_row = pl.multiple_of(place_ref[0] * coarse_rows, coarse_rows)
    own_first = pl.multiple_of(place_ref[1] * width, width)
    mate_first = pl.multiple_of((1 - place_ref[1]) * width, width)
    for slot in range(pair):
        target = pl.program_id(0) * pair + slot
        real_step = pltpu.roll(steps_ref[0], 128 - target, 1)[:, 0:1]
        imag_step = pltpu.roll(steps_ref[1], 128 - target, 1)[:, 0:1]
        far_real, far_imag = real_step[:coarse_rows], imag_step[:coarse_rows]
        low_real, low_imag = real_step[coarse_rows:], imag_step[coarse_rows:]
        coarse_real = coarse_ref[0, pl.ds(first_row, coarse_rows), :]
        coarse_imag = coarse_ref[1, pl.ds(first_row, coarse_rows), :]
        rows_ref[slot, 0] = far_real * coarse_real - far_imag * coarse_imag
        rows_ref[slot, 1] = far_real * coarse_imag + far_imag * coarse_real
        fine_real = low_real * fine_ref[0] - low_imag * fine_ref[1]
        fine_imag = low_real * fine_ref[1] + low_imag * fine_ref[0]
        for a in range(coarse_rows):
            row_real = rows_ref[slot, 0, pl.ds(a, 1), :]
            row_imag = rows_ref[slot, 1, pl.ds(a, 1), :]
            table_ref[slot, pl.ds(a * FINE, FINE), :columns] = (
                row_real * fine_real - row_imag * fine_imag
            ).astype(jnp.bfloat16)
            table_ref[slot, pl.ds(a * FINE, FINE), columns:] = (
                row_real * fine_imag + row_imag * fine_real
            ).astype(jnp.bfloat16)
    for slot in range(pair):
        total_real = jnp.zeros((row_count, columns), jnp.float32)
        total_imag = jnp.zeros((row_count, columns), jnp.float32)
        own_table = table_ref[slot, pl.ds(own_first, width), :]
        mate_table = table_ref[slot, pl.ds(mate_first, width), :]
        for number in range(window):
            own = own_ref[number].reshape(2 * row_count, width)
            mate = mate_ref[number].reshape(2 * row_count, width)
            product = jnp.dot(own, own_table, preferred_element_type=jnp.float32)
            product += jnp.dot(mate, mate_table, preferred_element_type=jnp.float32)
            real_part = product[:row_count, :columns] - product[row_count:, columns:]
            imag_part = product[:row_count, columns:] + product[row_count:, :columns]
            cosine = factor_ref[slot, 2 * number : 2 * number + 1, :]
            sine = factor_ref[slot, 2 * number + 1 : 2 * number + 2, :]
            total_real += real_part * cosine - imag_part * sine
            total_imag += real_part * sine + imag_part * cosine
        out_ref[slot, :, :columns] = total_real.astype(jnp.bfloat16)
        out_ref[slot, :, columns:] = total_imag.astype(jnp.bfloat16)


def predict(place, steps, factors, own, mate, columns):
    targets = factors.shape[0]
    row_count, width = own.shape[2:]
    pair = 2
    coarse = turn_table(np.arange(YB // FINE) * FINE, np.arange(columns))
    fine = turn_table(np.arange(FINE), np.arange(columns))
    whole = pl.BlockSpec(memory_space=pltpu.VMEM)
    return pl.pallas_call(
        predict_kernel,
        grid=(targets // pair,),
        out_shape=jax.ShapeDtypeStruct((targets, row_count, 2 * columns), jnp.bfloat16),
        in_specs=[
            pl.BlockSpec(memory_space=pltpu.SMEM),
            whole,
            whole,
            whole,
            pl.BlockSpec((pair, factors.shape[1], columns), lambda i: (i, 0, 0)),
            whole,
            whole,
        ],
        out_specs=pl.BlockSpec((pair, row_count, 2 * columns), lambda i: (i, 0, 0)),
        scratch_shapes=[
            pltpu.VMEM((pair, 2, 2 * width // FINE, columns), jnp.float32),
            pltpu.VMEM((pair, 2 * width, 2 * columns), jnp.bfloat16),
        ],
        compiler_params=pltpu.CompilerParams(vmem_limit_bytes=32 * 1024 * 1024),
    )(place, steps, coarse, fine, factors, own, mate)


def degrid_kernel(row_ref, col_ref, count_ref, own_ref, rim_ref, kernel_ref, out_ref, extended_ref, flipped_ref):
    columns = own_ref.shape[1] // 2
    row_count = own_ref.shape[0]
    extended_ref[:row_count] = own_ref[...]
    extended_ref[row_count : row_count + KS] = rim_ref[...]
    extended_ref[row_count + KS :] = jnp.zeros_like(extended_ref[row_count + KS :])
    flipped_ref[...] = extended_ref[...].T

    def group(g, carry):
        values = ([], [])
        for j in range(8):
            b = g * 8 + j
            first = row_ref[b]
            start = col_ref[b]
            live = b < count_ref[0]
            weights = kernel_ref[b].astype(jnp.float32)
            shift = lax.rem(128 - first, 128)
            for part in range(2):
                patch = flipped_ref[pl.ds(part * columns + start, KS), :]
                patch = pltpu.roll(patch, shift, 1)
                total = patch[:, 0:1] * weights[:KS]
                for a in range(1, KS):
                    total += patch[:, a : a + 1] * weights[a * KS : (a + 1) * KS]
                value = jnp.sum(total, axis=0, keepdims=True)
                values[part].append(jnp.where(live, value, 0.0))
        for part in range(2):
            out_ref[pl.ds(pl.multiple_of(g * 8, 8), 8), part * 128 : (part + 1) * 128] = (
                jnp.concatenate(values[part], axis=0)
            )
        return carry

    lax.fori_loop(0, kernel_ref.shape[0] // 8, group, 0)


def degrid(own, rim, kernel, row_starts, col_starts, live_count):
    whole = pl.BlockSpec(memory_space=pltpu.VMEM)
    scalar = pl.BlockSpec(memory_space=pltpu.SMEM)
    return pl.pallas_call(
        degrid_kernel,
        out_shape=jax.ShapeDtypeStruct((kernel.shape[0], 2 * kernel.shape[2]), jnp.float32),
        in_specs=[scalar, scalar, scalar, whole, whole, whole],
        out_specs=whole,
        scratch_shapes=[
            pltpu.VMEM((128, own.shape[1]), jnp.float32),
            pltpu.VMEM((own.shape[1], 128), jnp.float32),
        ],
        compiler_params=pltpu.CompilerParams(vmem_limit_bytes=32 * 1024 * 1024),
    )(row_starts, col_starts, live_count, own, rim, kernel)


def cos_sin(turns, sign):
    angles = turns.astype(jnp.float32) * (2.0 * math.pi / N_IMAGE)
    return jnp.cos(angles), sign * jnp.sin(angles)


def quad_groups(facets, subs):
    groups = []
    for core in range(2):
        for quad in range(facets // SPREAD):
            group = []
            for dz in range(SPREAD):
                z = (SPREAD * quad + SPREAD // 2 * core + dz) % facets
                group.extend(z * subs + s for s in range(core, subs, 2))
            groups.append(group)
    return groups


def on_device(facet_data, facet_taper, subgrid_offsets, kernels, block_row, block_col, block_count):
    facet_index = lax.axis_index("facet")
    sub_index = lax.axis_index("sub")
    facets = lax.axis_size("facet")
    subs = lax.axis_size("sub")
    vis_count = lax.axis_size("vis")
    columns = facet_taper.shape[1]
    row_count, width = facet_data.shape[2:]
    targets = SPREAD * subs // 2
    scale = 1.0 / math.sqrt(YB * facets)
    far_groups = [[j + SPREAD * k for k in range(facets // SPREAD)] for j in range(SPREAD)]
    own = lax.all_gather(facet_data[:, 0], "facet", axis_index_groups=far_groups)
    mate = lax.ppermute(own, "sub", [(s, s ^ 1) for s in range(subs)])

    core = sub_index % 2
    place = jnp.stack([sub_index // 2, core])
    half = SPREAD // 2 * core
    quad_first = (facet_index - half) // SPREAD * SPREAD + half
    members = jnp.arange(targets, dtype=jnp.int32)
    target_z = (quad_first + members // (subs // 2)) % facets
    target_s = members % (subs // 2) * 2 + core
    origin = (subgrid_offsets.reshape(-1)[target_z * subs + target_s] - columns // 2) % N_IMAGE
    multiples = jnp.concatenate(
        [
            sub_index // 2 * (2 * width) + jnp.arange(2 * width // FINE, dtype=jnp.int32) * FINE,
            jnp.arange(FINE, dtype=jnp.int32),
        ]
    )
    step_turns = (multiples[:, None] * origin[None, :]) % N_IMAGE
    step_turns = jnp.pad(step_turns, ((0, 0), (0, 128 - targets)))
    steps = jnp.stack(cos_sin(step_turns, -1.0))
    frequencies = (origin[:, None] + jnp.arange(columns, dtype=jnp.int32)[None, :]) % N_IMAGE
    window = facet_index % SPREAD + SPREAD * jnp.arange(facets // SPREAD, dtype=jnp.int32)
    shifts = window * YB % N_IMAGE
    phase_turns = (shifts[None, :, None] * (frequencies[:, None, :] % (N_IMAGE // YB))) % N_IMAGE
    cosine, sine = cos_sin(phase_turns, -1.0)
    weight = facet_taper[window] * scale
    factors = jnp.stack([weight[None] * cosine, weight[None] * sine], axis=2)
    factors = factors.reshape(targets, 2 * (facets // SPREAD), columns)

    partial = predict(place, steps, factors, own, mate, columns)
    received = lax.all_to_all(
        partial, ("facet", "sub"), 0, 0, axis_index_groups=quad_groups(facets, subs), tiled=True
    )
    summed = jnp.sum(received.astype(jnp.float32), axis=0)
    rim = lax.ppermute(summed[:KS], "vis", [(i, i - 1) for i in range(1, vis_count)])
    visibilities = degrid(
        summed, rim, kernels[0, 0, 0], block_row[0, 0, 0], block_col[0, 0, 0], block_count[0, 0]
    )
    return (
        summed.reshape(1, 1, row_count, 2 * columns),
        visibilities.reshape((1, 1, 1) + visibilities.shape),
    )


def solution(mesh):
    return jax.shard_map(
        on_device,
        mesh=mesh,
        in_specs=(
            P(None, "facet", "vis", "sub"),
            P(),
            P(),
            P("facet", "sub", "vis", None, None, None),
            P("facet", "sub", "vis", None),
            P("facet", "sub", "vis", None),
            P("facet", "sub", "vis"),
        ),
        out_specs=(P("facet", "sub", "vis", None), P("facet", "sub", "vis", None, None)),
        check_vma=False,
    )
```

```python
import math

import jax
import jax.numpy as jnp
import numpy as np
from jax import lax
from jax.experimental import pallas as pl
from jax.experimental.pallas import tpu as pltpu
from jax.sharding import PartitionSpec as P

N_IMAGE = 65536
YB = 2048
KS = 8
FINE = 32
WINDOW = 4


def turn_table(left, right):
    turns = (left.astype(np.int64)[:, None] * right.astype(np.int64)[None, :]) % N_IMAGE
    angles = turns * (2.0 * math.pi / N_IMAGE)
    return np.stack([np.cos(angles), -np.sin(angles)]).astype(np.float32)


def predict_kernel(core_ref, steps_ref, coarse_ref, fine_ref, factor_ref, own_ref, mate_ref, out_ref, rows_ref, table_ref):
    columns = coarse_ref.shape[2]
    chips, window, _, row_count, width = own_ref.shape
    pair = out_ref.shape[0]
    block_rows = width // FINE
    coarse_rows = coarse_ref.shape[1]
    for slot in range(pair):
        target = pl.program_id(0) * pair + slot
        real_step = pltpu.roll(steps_ref[0], 128 - target, 1)[:, 0:1]
        imag_step = pltpu.roll(steps_ref[1], 128 - target, 1)[:, 0:1]
        far_real, far_imag = real_step[:coarse_rows], imag_step[:coarse_rows]
        low_real, low_imag = real_step[coarse_rows:], imag_step[coarse_rows:]
        rows_ref[slot, 0] = far_real * coarse_ref[0] - far_imag * coarse_ref[1]
        rows_ref[slot, 1] = far_real * coarse_ref[1] + far_imag * coarse_ref[0]
        fine_real = low_real * fine_ref[0] - low_imag * fine_ref[1]
        fine_imag = low_real * fine_ref[1] + low_imag * fine_ref[0]
        for chip in range(chips):
            for side in range(2):
                core = core_ref[0] if side == 0 else 1 - core_ref[0]
                for a in range(block_rows):
                    row = (2 * chip + core) * block_rows + a
                    first = ((2 * chip + side) * block_rows + a) * FINE
                    row_real = rows_ref[slot, 0, pl.ds(row, 1), :]
                    row_imag = rows_ref[slot, 1, pl.ds(row, 1), :]
                    table_ref[slot, pl.ds(first, FINE), :columns] = (
                        row_real * fine_real - row_imag * fine_imag
                    ).astype(jnp.bfloat16)
                    table_ref[slot, pl.ds(first, FINE), columns:] = (
                        row_real * fine_imag + row_imag * fine_real
                    ).astype(jnp.bfloat16)
    samples = []
    for chip in range(chips):
        samples.append(own_ref[chip].reshape(window * 2 * row_count, width))
        samples.append(mate_ref[chip].reshape(window * 2 * row_count, width))
    samples = jnp.concatenate(samples, axis=1)
    for slot in range(pair):
        products = jnp.dot(samples, table_ref[slot], preferred_element_type=jnp.float32)
        products = products.reshape(window, 2 * row_count, 2 * columns)
        total_real = jnp.zeros((row_count, columns), jnp.float32)
        total_imag = jnp.zeros((row_count, columns), jnp.float32)
        for number in range(window):
            product = products[number]
            real_part = product[:row_count, :columns] - product[row_count:, columns:]
            imag_part = product[:row_count, columns:] + product[row_count:, :columns]
            cosine = factor_ref[slot, 2 * number : 2 * number + 1, :]
            sine = factor_ref[slot, 2 * number + 1 : 2 * number + 2, :]
            total_real += real_part * cosine - imag_part * sine
            total_imag += real_part * sine + imag_part * cosine
        out_ref[slot, :, :columns] = total_real.astype(jnp.bfloat16)
        out_ref[slot, :, columns:] = total_imag.astype(jnp.bfloat16)


def predict(core, steps, factors, own, mate, columns):
    targets = factors.shape[0]
    row_count = own.shape[3]
    pair = 2
    coarse = turn_table(np.arange(YB // FINE) * FINE, np.arange(columns))
    fine = turn_table(np.arange(FINE), np.arange(columns))
    whole = pl.BlockSpec(memory_space=pltpu.VMEM)
    return pl.pallas_call(
        predict_kernel,
        grid=(targets // pair,),
        out_shape=jax.ShapeDtypeStruct((targets, row_count, 2 * columns), jnp.bfloat16),
        in_specs=[
            pl.BlockSpec(memory_space=pltpu.SMEM),
            whole,
            whole,
            whole,
            pl.BlockSpec((pair, factors.shape[1], columns), lambda i: (i, 0, 0)),
            whole,
            whole,
        ],
        out_specs=pl.BlockSpec((pair, row_count, 2 * columns), lambda i: (i, 0, 0)),
        scratch_shapes=[
            pltpu.VMEM((pair, 2, YB // FINE, columns), jnp.float32),
            pltpu.VMEM((pair, YB, 2 * columns), jnp.bfloat16),
        ],
        compiler_params=pltpu.CompilerParams(vmem_limit_bytes=32 * 1024 * 1024),
    )(core, steps, coarse, fine, factors, own, mate)


def degrid_kernel(row_ref, col_ref, count_ref, own_ref, rim_ref, kernel_ref, out_ref, tiles_ref):
    columns = own_ref.shape[1] // 2
    row_count = own_ref.shape[0]
    taps = kernel_ref.shape[1]
    for part in range(2):
        for tile in range(3):
            first = part * columns + tile * 64
            tiles_ref[3 * part + tile, :row_count] = own_ref[:, first : first + 128]
            tiles_ref[3 * part + tile, row_count:] = rim_ref[:, first : first + 128]
    row_at = lax.broadcasted_iota(jnp.int32, (8, 128), 0)
    lane_at = lax.broadcasted_iota(jnp.int32, (8, 128), 1)
    tap_masks = [lane_at // KS == row_at + 8 * half for half in range(2)]
    half_at = lane_at // 64
    tap_at = lane_at % KS

    def group(g, carry):
        parts = []
        for quad in range(2):
            spread = []
            for tile in range(2):
                sums = []
                for part in range(2):
                    merged = jnp.zeros((8, 128), jnp.float32)
                    for half in range(2):
                        b = g * 8 + quad * 4 + tile * 2 + half
                        start = col_ref[b]
                        cut = (start > 120).astype(jnp.int32) + (start > 184).astype(jnp.int32)
                        patch = tiles_ref[3 * part + cut, pl.ds(row_ref[b], KS), :]
                        picks = tap_at + (start - 64 * cut)
                        patch = jnp.take_along_axis(patch, picks, axis=1, mode="promise_in_bounds")
                        merged = jnp.where(tap_masks[half], patch, merged)
                    sums.append(jnp.sum(merged, axis=0, keepdims=True))
                wanted = half_at + 2 * tile
                value = jnp.where(row_at == wanted, sums[0], 0.0)
                spread.append(jnp.where(row_at == wanted + 4, sums[1], value))
            weights = kernel_ref[pl.ds(g * 8 + quad * 4, 4)].reshape(4 * taps, 128)
            exact = jnp.concatenate(spread, axis=1)
            high = exact.astype(jnp.bfloat16)
            low = (exact - high.astype(jnp.float32)).astype(jnp.bfloat16)
            stacked = jnp.concatenate([high, low], axis=0)
            product = jnp.dot(stacked, weights, preferred_element_type=jnp.float32)
            parts.append(product[:8] + product[8:])
        live = g * 8 + row_at < count_ref[0]
        for part in range(2):
            value = jnp.concatenate([p[4 * part : 4 * part + 4] for p in parts], axis=0)
            out_ref[pl.ds(pl.multiple_of(g * 8, 8), 8), part * 128 : (part + 1) * 128] = jnp.where(
                live, value, 0.0
            )
        return carry

    lax.fori_loop(0, kernel_ref.shape[0] // 8, group, 0, unroll=2)


def degrid(own, rim, kernel, row_starts, col_starts, live_count):
    whole = pl.BlockSpec(memory_space=pltpu.VMEM)
    scalar = pl.BlockSpec(memory_space=pltpu.SMEM)
    return pl.pallas_call(
        degrid_kernel,
        out_shape=jax.ShapeDtypeStruct((kernel.shape[0], 2 * kernel.shape[2]), jnp.float32),
        in_specs=[scalar, scalar, scalar, whole, whole, whole],
        out_specs=whole,
        scratch_shapes=[pltpu.VMEM((6, own.shape[0] + KS, 128), jnp.float32)],
        compiler_params=pltpu.CompilerParams(vmem_limit_bytes=32 * 1024 * 1024),
    )(row_starts, col_starts, live_count, own, rim, kernel)


def cos_sin(turns, sign):
    angles = turns.astype(jnp.float32) * (2.0 * math.pi / N_IMAGE)
    return jnp.cos(angles), sign * jnp.sin(angles)


def on_device(facet_data, facet_taper, subgrid_offsets, kernels, block_row, block_col, block_count):
    facet_index = lax.axis_index("facet")
    sub_index = lax.axis_index("sub")
    facets = lax.axis_size("facet")
    subs = lax.axis_size("sub")
    vis_count = lax.axis_size("vis")
    columns = facet_taper.shape[1]
    row_count, width = facet_data.shape[2:]
    targets = facets // WINDOW
    scale = 1.0 / math.sqrt(YB * facets)
    near_groups = [[WINDOW * j + k for k in range(WINDOW)] for j in range(targets)]
    far_groups = [[j + WINDOW * k for k in range(targets)] for j in range(WINDOW)]
    core_groups = [list(range(core, subs, 2)) for core in range(2)]
    near = lax.all_gather(facet_data[:, 0], "facet", axis_index_groups=near_groups)
    copies = jnp.broadcast_to(near[None], (subs // 2,) + near.shape)
    own = lax.all_to_all(copies, "sub", 0, 0, axis_index_groups=core_groups)
    mate = lax.ppermute(own, "sub", [(s, s ^ 1) for s in range(subs)])

    chosen = facet_index % WINDOW + WINDOW * jnp.arange(targets, dtype=jnp.int32)
    origin = (subgrid_offsets[chosen, sub_index] - columns // 2) % N_IMAGE
    multiples = jnp.concatenate(
        [jnp.arange(YB // FINE, dtype=jnp.int32) * FINE, jnp.arange(FINE, dtype=jnp.int32)]
    )
    step_turns = (multiples[:, None] * origin[None, :]) % N_IMAGE
    step_turns = jnp.pad(step_turns, ((0, 0), (0, 128 - targets)))
    steps = jnp.stack(cos_sin(step_turns, -1.0))
    frequencies = (origin[:, None] + jnp.arange(columns, dtype=jnp.int32)[None, :]) % N_IMAGE
    window = facet_index // WINDOW * WINDOW + jnp.arange(WINDOW, dtype=jnp.int32)
    shifts = window * YB % N_IMAGE
    phase_turns = (shifts[None, :, None] * (frequencies[:, None, :] % (N_IMAGE // YB))) % N_IMAGE
    cosine, sine = cos_sin(phase_turns, -1.0)
    weight = facet_taper[window] * scale
    factors = jnp.stack([weight[None] * cosine, weight[None] * sine], axis=2)
    factors = factors.reshape(targets, 2 * WINDOW, columns)

    core = (sub_index % 2).reshape(1)
    partial = predict(core, steps, factors, own, mate, columns)
    received = lax.all_to_all(partial, "facet", 0, 0, axis_index_groups=far_groups, tiled=True)
    summed = jnp.sum(received.astype(jnp.float32), axis=0)
    rim = lax.ppermute(summed[:KS], "vis", [(i, i - 1) for i in range(1, vis_count)])
    visibilities = degrid(
        summed, rim, kernels[0, 0, 0], block_row[0, 0, 0], block_col[0, 0, 0], block_count[0, 0]
    )
    return (
        summed.reshape(1, 1, row_count, 2 * columns),
        visibilities.reshape((1, 1, 1) + visibilities.shape),
    )


def solution(mesh):
    return jax.shard_map(
        on_device,
        mesh=mesh,
        in_specs=(
            P(None, "facet", "vis", "sub"),
            P(),
            P(),
            P("facet", "sub", "vis", None, None, None),
            P("facet", "sub", "vis", None),
            P("facet", "sub", "vis", None),
            P("facet", "sub", "vis"),
        ),
        out_specs=(P("facet", "sub", "vis", None), P("facet", "sub", "vis", None, None)),
        check_vma=False,
    )
```

```python
import math

import jax
import jax.numpy as jnp
import numpy as np
from jax import lax
from jax.experimental import pallas as pl
from jax.experimental.pallas import tpu as pltpu
from jax.sharding import PartitionSpec as P

N_IMAGE = 65536
YB = 2048
KS = 8
FINE = 32
SPREAD = 4


def turn_table(left, right):
    turns = (left.astype(np.int64)[:, None] * right.astype(np.int64)[None, :]) % N_IMAGE
    angles = turns * (2.0 * math.pi / N_IMAGE)
    return np.stack([np.cos(angles), -np.sin(angles)]).astype(np.float32)


def predict_kernel(place_ref, steps_ref, coarse_ref, fine_ref, factor_ref, own_ref, mate_ref, out_ref, rows_ref, table_ref):
    columns = coarse_ref.shape[2]
    window, _, row_count, width = own_ref.shape
    pair = out_ref.shape[0]
    block_rows = width // FINE
    coarse_parts = []
    for part in range(2):
        sides = [
            coarse_ref[part, pl.ds(pl.multiple_of(place_ref[side] * block_rows, block_rows), block_rows), :]
            for side in range(2)
        ]
        coarse_parts.append(jnp.concatenate(sides, axis=0))
    coarse_real, coarse_imag = coarse_parts
    for slot in range(pair):
        target = pl.program_id(0) * pair + slot
        real_step = pltpu.roll(steps_ref[0], 128 - target, 1)[:, 0:1]
        imag_step = pltpu.roll(steps_ref[1], 128 - target, 1)[:, 0:1]
        far_real, far_imag = real_step[: 2 * block_rows], imag_step[: 2 * block_rows]
        low_real, low_imag = real_step[2 * block_rows :], imag_step[2 * block_rows :]
        rows_ref[slot, 0] = far_real * coarse_real - far_imag * coarse_imag
        rows_ref[slot, 1] = far_real * coarse_imag + far_imag * coarse_real
        fine_real = low_real * fine_ref[0] - low_imag * fine_ref[1]
        fine_imag = low_real * fine_ref[1] + low_imag * fine_ref[0]
        for a in range(2 * block_rows):
            row_real = rows_ref[slot, 0, pl.ds(a, 1), :]
            row_imag = rows_ref[slot, 1, pl.ds(a, 1), :]
            table_ref[slot, pl.ds(a * FINE, FINE), :columns] = (
                row_real * fine_real - row_imag * fine_imag
            ).astype(jnp.bfloat16)
            table_ref[slot, pl.ds(a * FINE, FINE), columns:] = (
                row_real * fine_imag + row_imag * fine_real
            ).astype(jnp.bfloat16)
    own = own_ref[...].reshape(window * 2 * row_count, width)
    mate = mate_ref[...].reshape(window * 2 * row_count, width)
    samples = jnp.concatenate([own, mate], axis=1)
    for slot in range(pair):
        products = jnp.dot(samples, table_ref[slot], preferred_element_type=jnp.float32)
        products = products.reshape(window, 2 * row_count, 2 * columns)
        total_real = jnp.zeros((row_count, columns), jnp.float32)
        total_imag = jnp.zeros((row_count, columns), jnp.float32)
        for number in range(window):
            product = products[number]
            real_part = product[:row_count, :columns] - product[row_count:, columns:]
            imag_part = product[:row_count, columns:] + product[row_count:, :columns]
            cosine = factor_ref[slot, 2 * number : 2 * number + 1, :]
            sine = factor_ref[slot, 2 * number + 1 : 2 * number + 2, :]
            total_real += real_part * cosine - imag_part * sine
            total_imag += real_part * sine + imag_part * cosine
        out_ref[slot, :, :columns] = total_real.astype(jnp.bfloat16)
        out_ref[slot, :, columns:] = total_imag.astype(jnp.bfloat16)


def predict(place, steps, factors, own, mate, columns):
    targets = factors.shape[0]
    row_count, width = own.shape[2:]
    pair = 2
    coarse = turn_table(np.arange(YB // FINE) * FINE, np.arange(columns))
    fine = turn_table(np.arange(FINE), np.arange(columns))
    whole = pl.BlockSpec(memory_space=pltpu.VMEM)
    return pl.pallas_call(
        predict_kernel,
        grid=(targets // pair,),
        out_shape=jax.ShapeDtypeStruct((targets, row_count, 2 * columns), jnp.bfloat16),
        in_specs=[
            pl.BlockSpec(memory_space=pltpu.SMEM),
            whole,
            whole,
            whole,
            pl.BlockSpec((pair, factors.shape[1], columns), lambda i: (i, 0, 0)),
            whole,
            whole,
        ],
        out_specs=pl.BlockSpec((pair, row_count, 2 * columns), lambda i: (i, 0, 0)),
        scratch_shapes=[
            pltpu.VMEM((pair, 2, 2 * width // FINE, columns), jnp.float32),
            pltpu.VMEM((pair, 2 * width, 2 * columns), jnp.bfloat16),
        ],
        compiler_params=pltpu.CompilerParams(vmem_limit_bytes=32 * 1024 * 1024),
    )(place, steps, coarse, fine, factors, own, mate)


def degrid_kernel(row_ref, col_ref, count_ref, own_ref, rim_ref, kernel_ref, out_ref, tiles_ref):
    columns = own_ref.shape[1] // 2
    row_count = own_ref.shape[0]
    taps = kernel_ref.shape[1]
    for part in range(2):
        for tile in range(3):
            first = part * columns + tile * 64
            tiles_ref[3 * part + tile, :row_count] = own_ref[:, first : first + 128]
            tiles_ref[3 * part + tile, row_count:] = rim_ref[:, first : first + 128]
    row_at = lax.broadcasted_iota(jnp.int32, (8, 128), 0)
    lane_at = lax.broadcasted_iota(jnp.int32, (8, 128), 1)
    tap_masks = [lane_at // KS == row_at + 8 * half for half in range(2)]
    half_at = lane_at // 64
    tap_at = lane_at % KS

    def group(g, carry):
        parts = []
        for quad in range(2):
            spread = []
            for tile in range(2):
                sums = []
                for part in range(2):
                    merged = jnp.zeros((8, 128), jnp.float32)
                    for half in range(2):
                        b = g * 8 + quad * 4 + tile * 2 + half
                        start = col_ref[b]
                        cut = (start > 120).astype(jnp.int32) + (start > 184).astype(jnp.int32)
                        patch = tiles_ref[3 * part + cut, pl.ds(row_ref[b], KS), :]
                        picks = tap_at + (start - 64 * cut)
                        patch = jnp.take_along_axis(patch, picks, axis=1, mode="promise_in_bounds")
                        merged = jnp.where(tap_masks[half], patch, merged)
                    sums.append(jnp.sum(merged, axis=0, keepdims=True))
                wanted = half_at + 2 * tile
                value = jnp.where(row_at == wanted, sums[0], 0.0)
                spread.append(jnp.where(row_at == wanted + 4, sums[1], value))
            weights = kernel_ref[pl.ds(g * 8 + quad * 4, 4)].reshape(4 * taps, 128)
            exact = jnp.concatenate(spread, axis=1)
            high = exact.astype(jnp.bfloat16)
            low = (exact - high.astype(jnp.float32)).astype(jnp.bfloat16)
            stacked = jnp.concatenate([high, low], axis=0)
            product = jnp.dot(stacked, weights, preferred_element_type=jnp.float32)
            parts.append(product[:8] + product[8:])
        live = g * 8 + row_at < count_ref[0]
        for part in range(2):
            value = jnp.concatenate([p[4 * part : 4 * part + 4] for p in parts], axis=0)
            out_ref[pl.ds(pl.multiple_of(g * 8, 8), 8), part * 128 : (part + 1) * 128] = jnp.where(
                live, value, 0.0
            )
        return carry

    lax.fori_loop(0, kernel_ref.shape[0] // 8, group, 0, unroll=2)


def degrid(own, rim, kernel, row_starts, col_starts, live_count):
    whole = pl.BlockSpec(memory_space=pltpu.VMEM)
    scalar = pl.BlockSpec(memory_space=pltpu.SMEM)
    return pl.pallas_call(
        degrid_kernel,
        out_shape=jax.ShapeDtypeStruct((kernel.shape[0], 2 * kernel.shape[2]), jnp.float32),
        in_specs=[scalar, scalar, scalar, whole, whole, whole],
        out_specs=whole,
        scratch_shapes=[pltpu.VMEM((6, own.shape[0] + KS, 128), jnp.float32)],
        compiler_params=pltpu.CompilerParams(vmem_limit_bytes=32 * 1024 * 1024),
    )(row_starts, col_starts, live_count, own, rim, kernel)


def cos_sin(turns, sign):
    angles = turns.astype(jnp.float32) * (2.0 * math.pi / N_IMAGE)
    return jnp.cos(angles), sign * jnp.sin(angles)


def quad_groups(facets, subs):
    groups = []
    for core in range(2):
        for quad in range(facets // SPREAD):
            group = []
            for dz in range(SPREAD):
                z = (SPREAD * quad + SPREAD // 2 * core + dz) % facets
                group.extend(z * subs + s for s in range(core, subs, 2))
            groups.append(group)
    return groups


def on_device(facet_data, facet_taper, subgrid_offsets, kernels, block_row, block_col, block_count):
    facet_index = lax.axis_index("facet")
    sub_index = lax.axis_index("sub")
    facets = lax.axis_size("facet")
    subs = lax.axis_size("sub")
    vis_count = lax.axis_size("vis")
    columns = facet_taper.shape[1]
    row_count, width = facet_data.shape[2:]
    targets = SPREAD * subs // 2
    scale = 1.0 / math.sqrt(YB * facets)
    far_groups = [[j + SPREAD * k for k in range(facets // SPREAD)] for j in range(SPREAD)]
    own = lax.all_gather(facet_data[:, 0], "facet", axis_index_groups=far_groups)
    mate = lax.ppermute(own, "sub", [(s, s ^ 1) for s in range(subs)])

    core = sub_index % 2
    place = jnp.stack([sub_index, sub_index ^ 1])
    half = SPREAD // 2 * core
    quad_first = (facet_index - half) // SPREAD * SPREAD + half
    members = jnp.arange(targets, dtype=jnp.int32)
    target_z = (quad_first + members // (subs // 2)) % facets
    target_s = members % (subs // 2) * 2 + core
    origin = (subgrid_offsets.reshape(-1)[target_z * subs + target_s] - columns // 2) % N_IMAGE
    multiples = jnp.concatenate(
        [
            sub_index * width + jnp.arange(width // FINE, dtype=jnp.int32) * FINE,
            (sub_index ^ 1) * width + jnp.arange(width // FINE, dtype=jnp.int32) * FINE,
            jnp.arange(FINE, dtype=jnp.int32),
        ]
    )
    step_turns = (multiples[:, None] * origin[None, :]) % N_IMAGE
    step_turns = jnp.pad(step_turns, ((0, 0), (0, 128 - targets)))
    steps = jnp.stack(cos_sin(step_turns, -1.0))
    frequencies = (origin[:, None] + jnp.arange(columns, dtype=jnp.int32)[None, :]) % N_IMAGE
    window = facet_index % SPREAD + SPREAD * jnp.arange(facets // SPREAD, dtype=jnp.int32)
    shifts = window * YB % N_IMAGE
    phase_turns = (shifts[None, :, None] * (frequencies[:, None, :] % (N_IMAGE // YB))) % N_IMAGE
    cosine, sine = cos_sin(phase_turns, -1.0)
    weight = facet_taper[window] * scale
    factors = jnp.stack([weight[None] * cosine, weight[None] * sine], axis=2)
    factors = factors.reshape(targets, 2 * (facets // SPREAD), columns)

    partial = predict(place, steps, factors, own, mate, columns)
    received = lax.all_to_all(
        partial, ("facet", "sub"), 0, 0, axis_index_groups=quad_groups(facets, subs), tiled=True
    )
    summed = jnp.sum(received.astype(jnp.float32), axis=0)
    rim = lax.ppermute(summed[:KS], "vis", [(i, i - 1) for i in range(1, vis_count)])
    visibilities = degrid(
        summed, rim, kernels[0, 0, 0], block_row[0, 0, 0], block_col[0, 0, 0], block_count[0, 0]
    )
    return (
        summed.reshape(1, 1, row_count, 2 * columns),
        visibilities.reshape((1, 1, 1) + visibilities.shape),
    )


def solution(mesh):
    return jax.shard_map(
        on_device,
        mesh=mesh,
        in_specs=(
            P(None, "facet", "vis", "sub"),
            P(),
            P(),
            P("facet", "sub", "vis", None, None, None),
            P("facet", "sub", "vis", None),
            P("facet", "sub", "vis", None),
            P("facet", "sub", "vis"),
        ),
        out_specs=(P("facet", "sub", "vis", None), P("facet", "sub", "vis", None, None)),
        check_vma=False,
    )
```

```python
import math

import jax
import jax.numpy as jnp
import numpy as np
from jax import lax
from jax.experimental import pallas as pl
from jax.experimental.pallas import tpu as pltpu
from jax.sharding import PartitionSpec as P

N_IMAGE = 65536
YB = 2048
KS = 8
FINE = 32
NEAR = 2
TARGETS = 8


def turn_table(left, right):
    turns = (left.astype(np.int64)[:, None] * right.astype(np.int64)[None, :]) % N_IMAGE
    angles = turns * (2.0 * math.pi / N_IMAGE)
    return np.stack([np.cos(angles), -np.sin(angles)]).astype(np.float32)


def predict_kernel(place_ref, offset_ref, taper_ref, coarse_ref, fine_ref, own_ref, mate_ref, out_ref, steps_ref, rows_ref, table_ref):
    columns = coarse_ref.shape[2]
    window, _, row_count, width = own_ref.shape
    pair = out_ref.shape[0]
    targets = pair * pl.num_programs(0)
    facets, subs = offset_ref.shape
    block_rows = width // FINE
    near = facets // window
    z, sub = place_ref[0], place_ref[1]
    core = sub % 2
    z_first = (z + near - core) // near * near + core + facets - near

    def target_origin(target):
        row = (z_first + target // (subs // 2)) % facets
        column = target % (subs // 2) * 2 + core
        return (offset_ref[row, column] + N_IMAGE - columns // 2) % N_IMAGE

    @pl.when(pl.program_id(0) == 0)
    def _():
        lane = lax.broadcasted_iota(jnp.int32, steps_ref.shape[1:], 1)
        row = lax.broadcasted_iota(jnp.int32, steps_ref.shape[1:], 0)
        origins = jnp.zeros_like(lane)
        for target in range(TARGETS):
            origins = jnp.where(lane == target, target_origin(target), origins)
        own_step = sub * width + row * FINE
        mate_step = (sub + 1 - 2 * core) * width + (row - block_rows) * FINE
        multiples = jnp.where(
            row < block_rows, own_step, jnp.where(row < 2 * block_rows, mate_step, row - 2 * block_rows)
        )
        real_part, imag_part = cos_sin((multiples * origins) % N_IMAGE, -1.0)
        steps_ref[0] = real_part
        steps_ref[1] = imag_part

    coarse_parts = []
    for part in range(2):
        sides = [
            coarse_ref[part, pl.ds(pl.multiple_of(side * block_rows, block_rows), block_rows), :]
            for side in (sub, sub + 1 - 2 * core)
        ]
        coarse_parts.append(jnp.concatenate(sides, axis=0))
    coarse_real, coarse_imag = coarse_parts
    own = own_ref[...].reshape(window * 2 * row_count, width)
    mate = mate_ref[...].reshape(window * 2 * row_count, width)
    samples = jnp.concatenate([own, mate], axis=1)
    tapers = [taper_ref[pl.ds(near * number + z % near, 1), :] for number in range(window)]
    weight = jnp.concatenate(tapers, axis=0) * (1.0 / math.sqrt(YB * facets))
    facet = near * lax.broadcasted_iota(jnp.int32, (window, columns), 0) + z % near
    step = lax.broadcasted_iota(jnp.int32, (window, columns), 1)
    for slot in range(pair):
        target = pl.program_id(0) * pair + slot
        real_step = pltpu.roll(steps_ref[0], 128 - target, 1)[:, 0:1]
        imag_step = pltpu.roll(steps_ref[1], 128 - target, 1)[:, 0:1]
        far_real, far_imag = real_step[: 2 * block_rows], imag_step[: 2 * block_rows]
        low_real, low_imag = real_step[2 * block_rows :], imag_step[2 * block_rows :]
        rows_ref[slot, 0] = far_real * coarse_real - far_imag * coarse_imag
        rows_ref[slot, 1] = far_real * coarse_imag + far_imag * coarse_real
        fine_real = low_real * fine_ref[0] - low_imag * fine_ref[1]
        fine_imag = low_real * fine_ref[1] + low_imag * fine_ref[0]
        for a in range(2 * block_rows):
            row_real = rows_ref[slot, 0, pl.ds(a, 1), :]
            row_imag = rows_ref[slot, 1, pl.ds(a, 1), :]
            table_ref[slot, pl.ds(a * FINE, FINE), :columns] = (
                row_real * fine_real - row_imag * fine_imag
            ).astype(jnp.bfloat16)
            table_ref[slot, pl.ds(a * FINE, FINE), columns:] = (
                row_real * fine_imag + row_imag * fine_real
            ).astype(jnp.bfloat16)
        turns = (facet * YB * ((target_origin(target) + step) % (N_IMAGE // YB))) % N_IMAGE
        cosines, sines = cos_sin(turns, -1.0)
        cosines, sines = weight * cosines, weight * sines
        products = jnp.dot(samples, table_ref[slot], preferred_element_type=jnp.float32)
        products = products.reshape(window, 2 * row_count, 2 * columns)
        total_real = jnp.zeros((row_count, columns), jnp.float32)
        total_imag = jnp.zeros((row_count, columns), jnp.float32)
        for number in range(window):
            product = products[number]
            real_part = product[:row_count, :columns] - product[row_count:, columns:]
            imag_part = product[:row_count, columns:] + product[row_count:, :columns]
            cosine = cosines[number : number + 1]
            sine = sines[number : number + 1]
            total_real += real_part * cosine - imag_part * sine
            total_imag += real_part * sine + imag_part * cosine
        out_ref[slot, :, :columns] = total_real.astype(jnp.bfloat16)
        out_ref[slot, :, columns:] = total_imag.astype(jnp.bfloat16)


def predict(place, offsets, taper, own, mate, targets):
    columns = taper.shape[1]
    row_count, width = own.shape[2:]
    pair = 2
    coarse = turn_table(np.arange(YB // FINE) * FINE, np.arange(columns))
    fine = turn_table(np.arange(FINE), np.arange(columns))
    whole = pl.BlockSpec(memory_space=pltpu.VMEM)
    scalar = pl.BlockSpec(memory_space=pltpu.SMEM)
    return pl.pallas_call(
        predict_kernel,
        grid=(targets // pair,),
        out_shape=jax.ShapeDtypeStruct((targets, row_count, 2 * columns), jnp.bfloat16),
        in_specs=[scalar, scalar, whole, whole, whole, whole, whole],
        out_specs=pl.BlockSpec((pair, row_count, 2 * columns), lambda i: (i, 0, 0)),
        scratch_shapes=[
            pltpu.VMEM((2, 2 * width // FINE + FINE, 128), jnp.float32),
            pltpu.VMEM((pair, 2, 2 * width // FINE, columns), jnp.float32),
            pltpu.VMEM((pair, 2 * width, 2 * columns), jnp.bfloat16),
        ],
        compiler_params=pltpu.CompilerParams(vmem_limit_bytes=40 * 1024 * 1024),
    )(place, offsets, taper, coarse, fine, own, mate)


def degrid_kernel(row_ref, col_ref, count_ref, own_ref, rim_ref, kernel_ref, out_ref, tiles_ref):
    columns = own_ref.shape[1] // 2
    row_count = own_ref.shape[0]
    taps = kernel_ref.shape[1]
    for part in range(2):
        for tile in range(3):
            first = part * columns + tile * 64
            tiles_ref[3 * part + tile, :row_count] = own_ref[:, first : first + 128]
            tiles_ref[3 * part + tile, row_count:] = rim_ref[:, first : first + 128]
    row_at = lax.broadcasted_iota(jnp.int32, (8, 128), 0)
    lane_at = lax.broadcasted_iota(jnp.int32, (8, 128), 1)
    tap_masks = [lane_at // KS == row_at + 8 * half for half in range(2)]
    half_at = lane_at // 64
    tap_at = lane_at % KS

    def group(g, carry):
        parts = []
        for quad in range(2):
            spread = []
            for tile in range(2):
                sums = []
                for part in range(2):
                    merged = jnp.zeros((8, 128), jnp.float32)
                    for half in range(2):
                        b = g * 8 + quad * 4 + tile * 2 + half
                        start = col_ref[b]
                        cut = (start > 120).astype(jnp.int32) + (start > 184).astype(jnp.int32)
                        patch = tiles_ref[3 * part + cut, pl.ds(row_ref[b], KS), :]
                        picks = tap_at + (start - 64 * cut)
                        patch = jnp.take_along_axis(patch, picks, axis=1, mode="promise_in_bounds")
                        merged = jnp.where(tap_masks[half], patch, merged)
                    sums.append(jnp.sum(merged, axis=0, keepdims=True))
                wanted = half_at + 2 * tile
                value = jnp.where(row_at == wanted, sums[0], 0.0)
                spread.append(jnp.where(row_at == wanted + 4, sums[1], value))
            weights = kernel_ref[pl.ds(g * 8 + quad * 4, 4)].reshape(4 * taps, 128)
            exact = jnp.concatenate(spread, axis=1)
            high = exact.astype(jnp.bfloat16)
            low = (exact - high.astype(jnp.float32)).astype(jnp.bfloat16)
            stacked = jnp.concatenate([high, low], axis=0)
            product = jnp.dot(stacked, weights, preferred_element_type=jnp.float32)
            parts.append(product[:8] + product[8:])
        live = g * 8 + row_at < count_ref[0]
        for part in range(2):
            value = jnp.concatenate([p[4 * part : 4 * part + 4] for p in parts], axis=0)
            out_ref[pl.ds(pl.multiple_of(g * 8, 8), 8), part * 128 : (part + 1) * 128] = jnp.where(
                live, value, 0.0
            )
        return carry

    lax.fori_loop(0, kernel_ref.shape[0] // 8, group, 0, unroll=2)


def degrid(own, rim, kernel, row_starts, col_starts, live_count):
    whole = pl.BlockSpec(memory_space=pltpu.VMEM)
    scalar = pl.BlockSpec(memory_space=pltpu.SMEM)
    return pl.pallas_call(
        degrid_kernel,
        out_shape=jax.ShapeDtypeStruct((kernel.shape[0], 2 * kernel.shape[2]), jnp.float32),
        in_specs=[scalar, scalar, scalar, whole, whole, whole],
        out_specs=whole,
        scratch_shapes=[pltpu.VMEM((6, own.shape[0] + KS, 128), jnp.float32)],
        compiler_params=pltpu.CompilerParams(vmem_limit_bytes=32 * 1024 * 1024),
    )(row_starts, col_starts, live_count, own, rim, kernel)


def cos_sin(turns, sign):
    angles = turns.astype(jnp.float32) * (2.0 * math.pi / N_IMAGE)
    return jnp.cos(angles), sign * jnp.sin(angles)


def near_groups(facets, subs):
    groups = []
    for core in range(2):
        for number in range(facets // NEAR):
            group = []
            for dz in range(NEAR):
                z = (NEAR * number + core + dz) % facets
                group.extend(z * subs + s for s in range(core, subs, 2))
            groups.append(group)
    return groups


def on_device(facet_data, facet_taper, subgrid_offsets, kernels, block_row, block_col, block_count):
    facet_index = lax.axis_index("facet")
    sub_index = lax.axis_index("sub")
    facets = lax.axis_size("facet")
    subs = lax.axis_size("sub")
    vis_count = lax.axis_size("vis")
    columns = facet_taper.shape[1]
    row_count = facet_data.shape[2]
    far_groups = [[j + NEAR * k for k in range(facets // NEAR)] for j in range(NEAR)]
    own = lax.all_gather(facet_data[:, 0], "facet", axis_index_groups=far_groups)
    mate = lax.ppermute(own, "sub", [(s, s ^ 1) for s in range(subs)])
    place = jnp.stack([facet_index, sub_index])
    partial = predict(place, subgrid_offsets, facet_taper, own, mate, TARGETS)
    received = lax.all_to_all(
        partial, ("facet", "sub"), 0, 0, axis_index_groups=near_groups(facets, subs), tiled=True
    )
    summed = jnp.sum(received.astype(jnp.float32), axis=0)
    rim = lax.ppermute(summed[:KS], "vis", [(i, i - 1) for i in range(1, vis_count)])
    visibilities = degrid(
        summed, rim, kernels[0, 0, 0], block_row[0, 0, 0], block_col[0, 0, 0], block_count[0, 0]
    )
    return (
        summed.reshape(1, 1, row_count, 2 * columns),
        visibilities.reshape((1, 1, 1) + visibilities.shape),
    )


def solution(mesh):
    return jax.shard_map(
        on_device,
        mesh=mesh,
        in_specs=(
            P(None, "facet", "vis", "sub"),
            P(),
            P(),
            P("facet", "sub", "vis", None, None, None),
            P("facet", "sub", "vis", None),
            P("facet", "sub", "vis", None),
            P("facet", "sub", "vis"),
        ),
        out_specs=(P("facet", "sub", "vis", None), P("facet", "sub", "vis", None, None)),
        check_vma=False,
    )
```

```python
import math

import jax
import jax.numpy as jnp
import numpy as np
from jax import lax
from jax.experimental import pallas as pl
from jax.experimental.pallas import tpu as pltpu
from jax.sharding import PartitionSpec as P

N_IMAGE = 65536
YB = 2048
KS = 8
FINE = 32
NEAR = 2
TARGETS = 8


def turn_table(left, right):
    turns = (left.astype(np.int64)[:, None] * right.astype(np.int64)[None, :]) % N_IMAGE
    angles = turns * (2.0 * math.pi / N_IMAGE)
    return np.stack([np.cos(angles), -np.sin(angles)]).astype(np.float32)


def predict_kernel(place_ref, offset_ref, taper_ref, coarse_ref, fine_ref, own_ref, mate_ref, out_ref, steps_ref, rows_ref, table_ref, samples_ref):
    columns = coarse_ref.shape[2]
    window, _, row_count, width = own_ref.shape
    pair = out_ref.shape[0]
    targets = pair * pl.num_programs(0)
    facets, subs = offset_ref.shape
    block_rows = width // FINE
    near = facets // window
    z, sub = place_ref[0], place_ref[1]
    core = sub % 2
    z_first = (z + near - core) // near * near + core + facets - near

    def target_origin(target):
        row = (z_first + target // (subs // 2)) % facets
        column = target % (subs // 2) * 2 + core
        return (offset_ref[row, column] + N_IMAGE - columns // 2) % N_IMAGE

    @pl.when(pl.program_id(0) == 0)
    def _():
        lane = lax.broadcasted_iota(jnp.int32, steps_ref.shape[1:], 1)
        row = lax.broadcasted_iota(jnp.int32, steps_ref.shape[1:], 0)
        origins = jnp.zeros_like(lane)
        for target in range(TARGETS):
            origins = jnp.where(lane == target, target_origin(target), origins)
        own_step = sub * width + row * FINE
        mate_step = (sub + 1 - 2 * core) * width + (row - block_rows) * FINE
        multiples = jnp.where(
            row < block_rows, own_step, jnp.where(row < 2 * block_rows, mate_step, row - 2 * block_rows)
        )
        real_part, imag_part = cos_sin((multiples * origins) % N_IMAGE, -1.0)
        steps_ref[0] = real_part
        steps_ref[1] = imag_part
        for number in range(window):
            for side, ref in enumerate((own_ref, mate_ref)):
                rows = slice(2 * number * row_count, (2 * number + 1) * row_count)
                after = slice((2 * number + 1) * row_count, (2 * number + 2) * row_count)
                left = slice(side * width, (side + 1) * width)
                right = slice((2 + side) * width, (3 + side) * width)
                samples_ref[rows, left] = ref[number, 0]
                samples_ref[rows, right] = -ref[number, 1]
                samples_ref[after, left] = ref[number, 1]
                samples_ref[after, right] = ref[number, 0]

    coarse_parts = []
    for part in range(2):
        sides = [
            coarse_ref[part, pl.ds(pl.multiple_of(side * block_rows, block_rows), block_rows), :]
            for side in (sub, sub + 1 - 2 * core)
        ]
        coarse_parts.append(jnp.concatenate(sides, axis=0))
    coarse_real, coarse_imag = coarse_parts
    tapers = [taper_ref[pl.ds(near * number + z % near, 1), :] for number in range(window)]
    weight = jnp.concatenate(tapers, axis=0) * (1.0 / math.sqrt(YB * facets))
    facet = near * lax.broadcasted_iota(jnp.int32, (window, columns), 0) + z % near
    step = lax.broadcasted_iota(jnp.int32, (window, columns), 1)
    for slot in range(pair):
        target = pl.program_id(0) * pair + slot
        real_step = pltpu.roll(steps_ref[0], 128 - target, 1)[:, 0:1]
        imag_step = pltpu.roll(steps_ref[1], 128 - target, 1)[:, 0:1]
        far_real, far_imag = real_step[: 2 * block_rows], imag_step[: 2 * block_rows]
        low_real, low_imag = real_step[2 * block_rows :], imag_step[2 * block_rows :]
        rows_ref[slot, 0] = far_real * coarse_real - far_imag * coarse_imag
        rows_ref[slot, 1] = far_real * coarse_imag + far_imag * coarse_real
        fine_real = low_real * fine_ref[0] - low_imag * fine_ref[1]
        fine_imag = low_real * fine_ref[1] + low_imag * fine_ref[0]
        for a in range(2 * block_rows):
            row_real = rows_ref[slot, 0, pl.ds(a, 1), :]
            row_imag = rows_ref[slot, 1, pl.ds(a, 1), :]
            table_ref[slot, pl.ds(a * FINE, FINE), :] = (
                row_real * fine_real - row_imag * fine_imag
            ).astype(jnp.bfloat16)
            table_ref[slot, pl.ds(2 * width + a * FINE, FINE), :] = (
                row_real * fine_imag + row_imag * fine_real
            ).astype(jnp.bfloat16)
        turns = (facet * YB * ((target_origin(target) + step) % (N_IMAGE // YB))) % N_IMAGE
        cosines, sines = cos_sin(turns, -1.0)
        cosines, sines = weight * cosines, weight * sines
        products = jnp.dot(samples_ref[...], table_ref[slot], preferred_element_type=jnp.float32)
        products = products.reshape(window, 2, row_count, columns)
        total_real = jnp.zeros((row_count, columns), jnp.float32)
        total_imag = jnp.zeros((row_count, columns), jnp.float32)
        for number in range(window):
            real_part = products[number, 0]
            imag_part = products[number, 1]
            cosine = cosines[number : number + 1]
            sine = sines[number : number + 1]
            total_real += real_part * cosine - imag_part * sine
            total_imag += real_part * sine + imag_part * cosine
        out_ref[slot, :, :columns] = total_real.astype(jnp.bfloat16)
        out_ref[slot, :, columns:] = total_imag.astype(jnp.bfloat16)


def predict(place, offsets, taper, own, mate, targets):
    columns = taper.shape[1]
    row_count, width = own.shape[2:]
    pair = 8
    coarse = turn_table(np.arange(YB // FINE) * FINE, np.arange(columns))
    fine = turn_table(np.arange(FINE), np.arange(columns))
    whole = pl.BlockSpec(memory_space=pltpu.VMEM)
    scalar = pl.BlockSpec(memory_space=pltpu.SMEM)
    return pl.pallas_call(
        predict_kernel,
        grid=(targets // pair,),
        out_shape=jax.ShapeDtypeStruct((targets, row_count, 2 * columns), jnp.bfloat16),
        in_specs=[scalar, scalar, whole, whole, whole, whole, whole],
        out_specs=pl.BlockSpec((pair, row_count, 2 * columns), lambda i: (i, 0, 0)),
        scratch_shapes=[
            pltpu.VMEM((2, 2 * width // FINE + FINE, 128), jnp.float32),
            pltpu.VMEM((pair, 2, 2 * width // FINE, columns), jnp.float32),
            pltpu.VMEM((pair, 4 * width, columns), jnp.bfloat16),
            pltpu.VMEM((own.shape[0] * 2 * row_count, 4 * width), jnp.bfloat16),
        ],
        compiler_params=pltpu.CompilerParams(vmem_limit_bytes=28 * 1024 * 1024),
    )(place, offsets, taper, coarse, fine, own, mate)


def degrid_kernel(place_ref, own_ref, rim_ref, kernel_ref, out_ref, tiles_ref):
    columns = own_ref.shape[1] // 2
    row_count = own_ref.shape[0]
    blocks, taps = kernel_ref.shape[:2]
    for part in range(2):
        for tile in range(3):
            first = part * columns + tile * 64
            tiles_ref[3 * part + tile, :row_count] = own_ref[:, first : first + 128]
            tiles_ref[3 * part + tile, row_count:] = rim_ref[:, first : first + 128]
    row_at = lax.broadcasted_iota(jnp.int32, (8, 128), 0)
    lane_at = lax.broadcasted_iota(jnp.int32, (8, 128), 1)
    tap_masks = [lane_at // KS == row_at + 8 * half for half in range(2)]
    half_at = lane_at // 64
    tap_at = lane_at % KS

    def group(g, carry):
        parts = []
        for quad in range(2):
            spread = []
            for tile in range(2):
                sums = []
                for part in range(2):
                    merged = jnp.zeros((8, 128), jnp.float32)
                    for half in range(2):
                        b = g * 8 + quad * 4 + tile * 2 + half
                        start = place_ref[blocks + b]
                        cut = (start > 120).astype(jnp.int32) + (start > 184).astype(jnp.int32)
                        patch = tiles_ref[3 * part + cut, pl.ds(place_ref[b], KS), :]
                        picks = tap_at + (start - 64 * cut)
                        patch = jnp.take_along_axis(patch, picks, axis=1, mode="promise_in_bounds")
                        merged = jnp.where(tap_masks[half], patch, merged)
                    sums.append(jnp.sum(merged, axis=0, keepdims=True))
                wanted = half_at + 2 * tile
                value = jnp.where(row_at == wanted, sums[0], 0.0)
                spread.append(jnp.where(row_at == wanted + 4, sums[1], value))
            weights = kernel_ref[pl.ds(g * 8 + quad * 4, 4)].reshape(4 * taps, 128)
            exact = jnp.concatenate(spread, axis=1)
            high = exact.astype(jnp.bfloat16)
            low = (exact - high.astype(jnp.float32)).astype(jnp.bfloat16)
            stacked = jnp.concatenate([high, low], axis=0)
            product = jnp.dot(stacked, weights, preferred_element_type=jnp.float32)
            parts.append(product[:8] + product[8:])
        live = g * 8 + row_at < place_ref[2 * blocks]
        for part in range(2):
            value = jnp.concatenate([p[4 * part : 4 * part + 4] for p in parts], axis=0)
            out_ref[pl.ds(pl.multiple_of(g * 8, 8), 8), part * 128 : (part + 1) * 128] = jnp.where(
                live, value, 0.0
            )
        return carry

    lax.fori_loop(0, kernel_ref.shape[0] // 8, group, 0, unroll=2)


def degrid(places, own, rim, kernel):
    whole = pl.BlockSpec(memory_space=pltpu.VMEM)
    scalar = pl.BlockSpec(memory_space=pltpu.SMEM)
    return pl.pallas_call(
        degrid_kernel,
        out_shape=jax.ShapeDtypeStruct((kernel.shape[0], 2 * kernel.shape[2]), jnp.float32),
        in_specs=[scalar, whole, whole, whole],
        out_specs=whole,
        scratch_shapes=[pltpu.VMEM((6, own.shape[0] + KS, 128), jnp.float32)],
        compiler_params=pltpu.CompilerParams(vmem_limit_bytes=32 * 1024 * 1024),
    )(places, own, rim, kernel)


def cos_sin(turns, sign):
    angles = turns.astype(jnp.float32) * (2.0 * math.pi / N_IMAGE)
    return jnp.cos(angles), sign * jnp.sin(angles)


def near_groups(facets, subs):
    groups = []
    for core in range(2):
        for number in range(facets // NEAR):
            group = []
            for dz in range(NEAR):
                z = (NEAR * number + core + dz) % facets
                group.extend(z * subs + s for s in range(core, subs, 2))
            groups.append(group)
    return groups


def on_device(facet_data, facet_taper, subgrid_offsets, kernels, block_row, block_col, block_count):
    facet_index = lax.axis_index("facet")
    sub_index = lax.axis_index("sub")
    facets = lax.axis_size("facet")
    subs = lax.axis_size("sub")
    vis_count = lax.axis_size("vis")
    columns = facet_taper.shape[1]
    row_count = facet_data.shape[2]
    far_groups = [[j + NEAR * k for k in range(facets // NEAR)] for j in range(NEAR)]
    own = lax.all_gather(facet_data[:, 0], "facet", axis_index_groups=far_groups)
    mate = lax.ppermute(own, "sub", [(s, s ^ 1) for s in range(subs)])
    place = jnp.stack([facet_index, sub_index])
    places = jnp.concatenate([block_row[0, 0, 0], block_col[0, 0, 0], block_count[0, 0]])
    place, places = lax.optimization_barrier((place, places))
    partial = predict(place, subgrid_offsets, facet_taper, own, mate, TARGETS)
    received = lax.all_to_all(
        partial, ("facet", "sub"), 0, 0, axis_index_groups=near_groups(facets, subs), tiled=True
    )
    summed = jnp.sum(received.astype(jnp.float32), axis=0)
    rim = lax.ppermute(summed[:KS], "vis", [(i, i - 1) for i in range(1, vis_count)])
    visibilities = degrid(places, summed, rim, kernels[0, 0, 0])
    return (
        summed.reshape(1, 1, row_count, 2 * columns),
        visibilities.reshape((1, 1, 1) + visibilities.shape),
    )


def solution(mesh):
    return jax.shard_map(
        on_device,
        mesh=mesh,
        in_specs=(
            P(None, "facet", "vis", "sub"),
            P(),
            P(),
            P("facet", "sub", "vis", None, None, None),
            P("facet", "sub", "vis", None),
            P("facet", "sub", "vis", None),
            P("facet", "sub", "vis"),
        ),
        out_specs=(P("facet", "sub", "vis", None), P("facet", "sub", "vis", None, None)),
        check_vma=False,
    )
```

```python
import math

import jax
import jax.numpy as jnp
import numpy as np
from jax import lax
from jax.experimental import pallas as pl
from jax.experimental.pallas import tpu as pltpu
from jax.sharding import PartitionSpec as P

N_IMAGE = 65536
YB = 2048
KS = 8
FINE = 32
NEAR = 2


def turn_table(left, right):
    turns = (left.astype(np.int64)[:, None] * right.astype(np.int64)[None, :]) % N_IMAGE
    angles = turns * (2.0 * math.pi / N_IMAGE)
    return np.stack([np.cos(angles), -np.sin(angles)]).astype(np.float32)


def predict_kernel(place_ref, offset_ref, taper_ref, coarse_ref, fine_ref, data_ref, out_ref, steps_ref, rows_ref, table_ref, samples_ref):
    columns = coarse_ref.shape[2]
    quads, members, _, row_count, width = data_ref.shape
    window = quads * members // 2
    pair = out_ref.shape[0]
    facets, subs = offset_ref.shape
    near = facets // window
    depth = 2 * width
    coarse_rows = depth // FINE
    z, chip = place_ref[0], place_ref[1]

    def target_origin(target):
        row = z // near * near + target // subs
        return (offset_ref[row, target % subs] + N_IMAGE - columns // 2) % N_IMAGE

    @pl.when(pl.program_id(0) == 0)
    def _():
        lane = lax.broadcasted_iota(jnp.int32, steps_ref.shape[1:], 1)
        row = lax.broadcasted_iota(jnp.int32, steps_ref.shape[1:], 0)
        origins = jnp.zeros_like(lane)
        for target in range(near * subs):
            origins = jnp.where(lane == target, target_origin(target), origins)
        multiples = jnp.where(row < coarse_rows, chip * depth + row * FINE, row - coarse_rows)
        real_part, imag_part = cos_sin((multiples * origins) % N_IMAGE, -1.0)
        steps_ref[0] = real_part
        steps_ref[1] = imag_part
        for number in range(window):
            for side in range(2):
                rows = slice(2 * number * row_count, (2 * number + 1) * row_count)
                after = slice((2 * number + 1) * row_count, (2 * number + 2) * row_count)
                left = slice(side * width, (side + 1) * width)
                right = slice((2 + side) * width, (3 + side) * width)
                block = data_ref.at[number // 2, number % 2 * 2 + side]
                samples_ref[rows, left] = block[0]
                samples_ref[rows, right] = -block[1]
                samples_ref[after, left] = block[1]
                samples_ref[after, right] = block[0]

    first_row = pl.multiple_of(chip * coarse_rows, coarse_rows)
    coarse_real = coarse_ref[0, pl.ds(first_row, coarse_rows), :]
    coarse_imag = coarse_ref[1, pl.ds(first_row, coarse_rows), :]
    tapers = [taper_ref[pl.ds(near * number + z % near, 1), :] for number in range(window)]
    weight = jnp.concatenate(tapers, axis=0) * (1.0 / math.sqrt(YB * facets))
    facet = near * lax.broadcasted_iota(jnp.int32, (window, columns), 0) + z % near
    step = lax.broadcasted_iota(jnp.int32, (window, columns), 1)
    for slot in range(pair):
        target = pl.program_id(0) * pair + slot
        real_step = pltpu.roll(steps_ref[0], 128 - target, 1)[:, 0:1]
        imag_step = pltpu.roll(steps_ref[1], 128 - target, 1)[:, 0:1]
        far_real, far_imag = real_step[:coarse_rows], imag_step[:coarse_rows]
        low_real, low_imag = real_step[coarse_rows:], imag_step[coarse_rows:]
        rows_ref[slot, 0] = far_real * coarse_real - far_imag * coarse_imag
        rows_ref[slot, 1] = far_real * coarse_imag + far_imag * coarse_real
        fine_real = low_real * fine_ref[0] - low_imag * fine_ref[1]
        fine_imag = low_real * fine_ref[1] + low_imag * fine_ref[0]
        for a in range(coarse_rows):
            row_real = rows_ref[slot, 0, pl.ds(a, 1), :]
            row_imag = rows_ref[slot, 1, pl.ds(a, 1), :]
            table_ref[slot, pl.ds(a * FINE, FINE), :] = (
                row_real * fine_real - row_imag * fine_imag
            ).astype(jnp.bfloat16)
            table_ref[slot, pl.ds(depth + a * FINE, FINE), :] = (
                row_real * fine_imag + row_imag * fine_real
            ).astype(jnp.bfloat16)
        turns = (facet * YB * ((target_origin(target) + step) % (N_IMAGE // YB))) % N_IMAGE
        cosines, sines = cos_sin(turns, -1.0)
        cosines, sines = weight * cosines, weight * sines
        products = jnp.dot(samples_ref[...], table_ref[slot], preferred_element_type=jnp.float32)
        products = products.reshape(window, 2, row_count, columns)
        total_real = jnp.zeros((row_count, columns), jnp.float32)
        total_imag = jnp.zeros((row_count, columns), jnp.float32)
        for number in range(window):
            real_part = products[number, 0]
            imag_part = products[number, 1]
            cosine = cosines[number : number + 1]
            sine = sines[number : number + 1]
            total_real += real_part * cosine - imag_part * sine
            total_imag += real_part * sine + imag_part * cosine
        out_ref[slot, :, :columns] = total_real.astype(jnp.bfloat16)
        out_ref[slot, :, columns:] = total_imag.astype(jnp.bfloat16)


def predict(place, offsets, taper, data):
    columns = taper.shape[1]
    row_count, width = data.shape[3:]
    window = data.shape[0] * data.shape[1] // 2
    targets = taper.shape[0] // window * offsets.shape[1]
    pair = 8
    coarse = turn_table(np.arange(YB // FINE) * FINE, np.arange(columns))
    fine = turn_table(np.arange(FINE), np.arange(columns))
    whole = pl.BlockSpec(memory_space=pltpu.VMEM)
    scalar = pl.BlockSpec(memory_space=pltpu.SMEM)
    return pl.pallas_call(
        predict_kernel,
        grid=(targets // pair,),
        out_shape=jax.ShapeDtypeStruct((targets, row_count, 2 * columns), jnp.bfloat16),
        in_specs=[scalar, scalar, whole, whole, whole, whole],
        out_specs=pl.BlockSpec((pair, row_count, 2 * columns), lambda i: (i, 0, 0)),
        scratch_shapes=[
            pltpu.VMEM((2, 2 * width // FINE + FINE, 128), jnp.float32),
            pltpu.VMEM((pair, 2, 2 * width // FINE, columns), jnp.float32),
            pltpu.VMEM((pair, 4 * width, columns), jnp.bfloat16),
            pltpu.VMEM((window * 2 * row_count, 4 * width), jnp.bfloat16),
        ],
        compiler_params=pltpu.CompilerParams(vmem_limit_bytes=28 * 1024 * 1024),
    )(place, offsets, taper, coarse, fine, data)


def degrid_kernel(place_ref, own_ref, rim_ref, kernel_ref, out_ref, tiles_ref):
    columns = own_ref.shape[1] // 2
    row_count = own_ref.shape[0]
    blocks, taps = kernel_ref.shape[:2]
    for part in range(2):
        for tile in range(3):
            first = part * columns + tile * 64
            tiles_ref[3 * part + tile, :row_count] = own_ref[:, first : first + 128]
            tiles_ref[3 * part + tile, row_count:] = rim_ref[:, first : first + 128]
    row_at = lax.broadcasted_iota(jnp.int32, (8, 128), 0)
    lane_at = lax.broadcasted_iota(jnp.int32, (8, 128), 1)
    tap_masks = [lane_at // KS == row_at + 8 * half for half in range(2)]
    half_at = lane_at // 64
    tap_at = lane_at % KS

    def group(g, carry):
        parts = []
        for quad in range(2):
            spread = []
            for tile in range(2):
                sums = []
                for part in range(2):
                    merged = jnp.zeros((8, 128), jnp.float32)
                    for half in range(2):
                        b = g * 8 + quad * 4 + tile * 2 + half
                        start = place_ref[blocks + b]
                        cut = (start > 120).astype(jnp.int32) + (start > 184).astype(jnp.int32)
                        patch = tiles_ref[3 * part + cut, pl.ds(place_ref[b], KS), :]
                        picks = tap_at + (start - 64 * cut)
                        patch = jnp.take_along_axis(patch, picks, axis=1, mode="promise_in_bounds")
                        merged = jnp.where(tap_masks[half], patch, merged)
                    sums.append(jnp.sum(merged, axis=0, keepdims=True))
                wanted = half_at + 2 * tile
                value = jnp.where(row_at == wanted, sums[0], 0.0)
                spread.append(jnp.where(row_at == wanted + 4, sums[1], value))
            weights = kernel_ref[pl.ds(g * 8 + quad * 4, 4)].reshape(4 * taps, 128)
            exact = jnp.concatenate(spread, axis=1)
            high = exact.astype(jnp.bfloat16)
            low = (exact - high.astype(jnp.float32)).astype(jnp.bfloat16)
            stacked = jnp.concatenate([high, low], axis=0)
            product = jnp.dot(stacked, weights, preferred_element_type=jnp.float32)
            parts.append(product[:8] + product[8:])
        live = g * 8 + row_at < place_ref[2 * blocks]
        for part in range(2):
            value = jnp.concatenate([p[4 * part : 4 * part + 4] for p in parts], axis=0)
            out_ref[pl.ds(pl.multiple_of(g * 8, 8), 8), part * 128 : (part + 1) * 128] = jnp.where(
                live, value, 0.0
            )
        return carry

    lax.fori_loop(0, kernel_ref.shape[0] // 8, group, 0, unroll=2)


def degrid(places, own, rim, kernel):
    whole = pl.BlockSpec(memory_space=pltpu.VMEM)
    scalar = pl.BlockSpec(memory_space=pltpu.SMEM)
    return pl.pallas_call(
        degrid_kernel,
        out_shape=jax.ShapeDtypeStruct((kernel.shape[0], 2 * kernel.shape[2]), jnp.float32),
        in_specs=[scalar, whole, whole, whole],
        out_specs=whole,
        scratch_shapes=[pltpu.VMEM((6, own.shape[0] + KS, 128), jnp.float32)],
        compiler_params=pltpu.CompilerParams(vmem_limit_bytes=32 * 1024 * 1024),
    )(places, own, rim, kernel)


def cos_sin(turns, sign):
    angles = turns.astype(jnp.float32) * (2.0 * math.pi / N_IMAGE)
    return jnp.cos(angles), sign * jnp.sin(angles)


def on_device(facet_data, facet_taper, subgrid_offsets, kernels, block_row, block_col, block_count):
    facet_index = lax.axis_index("facet")
    sub_index = lax.axis_index("sub")
    facets = lax.axis_size("facet")
    subs = lax.axis_size("sub")
    vis_count = lax.axis_size("vis")
    columns = facet_taper.shape[1]
    row_count, width = facet_data.shape[2:]
    half_rows = row_count // 2
    place = jnp.stack([facet_index, sub_index // 2])
    places = jnp.concatenate([block_row[0, 0, 0], block_col[0, 0, 0], block_count[0, 0]])
    place, places = lax.optimization_barrier((place, places))
    pair_groups = [
        [z * subs + s + core for z in (first, first + NEAR) for core in range(2)]
        for quad in range(0, facets, 2 * NEAR)
        for first in range(quad, quad + NEAR)
        for s in range(0, subs, 2)
    ]
    far_groups = [list(range(j, facets, 2 * NEAR)) for j in range(2 * NEAR)]
    near_groups = [
        [z * subs + s for z in range(first, first + NEAR) for s in range(subs)]
        for first in range(0, facets, NEAR)
    ]
    halves = jnp.transpose(facet_data.reshape(2, 2, half_rows, width), (1, 0, 2, 3))
    copies = jnp.concatenate([halves, halves], axis=0)
    shared = lax.all_to_all(copies, ("facet", "sub"), 0, 0, axis_index_groups=pair_groups, tiled=True)
    data = lax.all_gather(shared, "facet", axis_index_groups=far_groups)
    partial = predict(place, subgrid_offsets, facet_taper, data)
    received = lax.all_to_all(
        partial, ("facet", "sub"), 0, 0, axis_index_groups=near_groups, tiled=True
    )
    received = received.reshape(NEAR * subs // 2, 2, half_rows, 2 * columns)
    summed = jnp.sum(received.astype(jnp.float32), axis=0).reshape(row_count, 2 * columns)
    rim = lax.ppermute(summed[:KS], "vis", [(i, i - 1) for i in range(1, vis_count)])
    visibilities = degrid(places, summed, rim, kernels[0, 0, 0])
    return (
        summed.reshape(1, 1, row_count, 2 * columns),
        visibilities.reshape((1, 1, 1) + visibilities.shape),
    )


def solution(mesh):
    return jax.shard_map(
        on_device,
        mesh=mesh,
        in_specs=(
            P(None, "facet", "vis", "sub"),
            P(),
            P(),
            P("facet", "sub", "vis", None, None, None),
            P("facet", "sub", "vis", None),
            P("facet", "sub", "vis", None),
            P("facet", "sub", "vis"),
        ),
        out_specs=(P("facet", "sub", "vis", None), P("facet", "sub", "vis", None, None)),
        check_vma=False,
    )
```

```python
import math

import jax
import jax.numpy as jnp
import numpy as np
from jax import lax
from jax.experimental import pallas as pl
from jax.experimental.pallas import tpu as pltpu
from jax.sharding import PartitionSpec as P

N_IMAGE = 65536
YB = 2048
KS = 8
FINE = 32
NEAR = 4


def turn_table(left, right):
    turns = (left.astype(np.int64)[:, None] * right.astype(np.int64)[None, :]) % N_IMAGE
    angles = turns * (2.0 * math.pi / N_IMAGE)
    return np.stack([np.cos(angles), -np.sin(angles)]).astype(np.float32)


def predict_kernel(place_ref, offset_ref, taper_ref, coarse_ref, fine_ref, data_ref, out_ref, steps_ref, rows_ref, table_ref, samples_ref):
    columns = coarse_ref.shape[2]
    members, _, row_count, width = data_ref.shape
    window = members // 2
    pair = out_ref.shape[0]
    facets, subs = offset_ref.shape
    near = facets // window
    depth = 2 * width
    coarse_rows = depth // FINE
    z, chip, core = place_ref[0], place_ref[1], place_ref[2]
    ahead = near // 2 * core
    z_first = (z + near - ahead) // near * near + ahead + facets - near

    def target_origin(target):
        row = (z_first + target // (subs // 2)) % facets
        column = target % (subs // 2) * 2 + core
        return (offset_ref[row, column] + N_IMAGE - columns // 2) % N_IMAGE

    @pl.when(pl.program_id(0) == 0)
    def _():
        lane = lax.broadcasted_iota(jnp.int32, steps_ref.shape[1:], 1)
        row = lax.broadcasted_iota(jnp.int32, steps_ref.shape[1:], 0)
        origins = jnp.zeros_like(lane)
        for target in range(near * subs // 2):
            origins = jnp.where(lane == target, target_origin(target), origins)
        multiples = jnp.where(row < coarse_rows, chip * depth + row * FINE, row - coarse_rows)
        real_part, imag_part = cos_sin((multiples * origins) % N_IMAGE, -1.0)
        steps_ref[0] = real_part
        steps_ref[1] = imag_part
        for number in range(window):
            for side in range(2):
                rows = slice(2 * number * row_count, (2 * number + 1) * row_count)
                after = slice((2 * number + 1) * row_count, (2 * number + 2) * row_count)
                left = slice(side * width, (side + 1) * width)
                right = slice((2 + side) * width, (3 + side) * width)
                block = data_ref.at[2 * number + side]
                samples_ref[rows, left] = block[0]
                samples_ref[rows, right] = -block[1]
                samples_ref[after, left] = block[1]
                samples_ref[after, right] = block[0]

    first_row = pl.multiple_of(chip * coarse_rows, coarse_rows)
    coarse_real = coarse_ref[0, pl.ds(first_row, coarse_rows), :]
    coarse_imag = coarse_ref[1, pl.ds(first_row, coarse_rows), :]
    tapers = [taper_ref[pl.ds(near * number + z % near, 1), :] for number in range(window)]
    weight = jnp.concatenate(tapers, axis=0) * (1.0 / math.sqrt(YB * facets))
    facet = near * lax.broadcasted_iota(jnp.int32, (window, columns), 0) + z % near
    step = lax.broadcasted_iota(jnp.int32, (window, columns), 1)
    for slot in range(pair):
        target = pl.program_id(0) * pair + slot
        real_step = pltpu.roll(steps_ref[0], 128 - target, 1)[:, 0:1]
        imag_step = pltpu.roll(steps_ref[1], 128 - target, 1)[:, 0:1]
        far_real, far_imag = real_step[:coarse_rows], imag_step[:coarse_rows]
        low_real, low_imag = real_step[coarse_rows:], imag_step[coarse_rows:]
        rows_ref[slot, 0] = far_real * coarse_real - far_imag * coarse_imag
        rows_ref[slot, 1] = far_real * coarse_imag + far_imag * coarse_real
        fine_real = low_real * fine_ref[0] - low_imag * fine_ref[1]
        fine_imag = low_real * fine_ref[1] + low_imag * fine_ref[0]
        for a in range(coarse_rows):
            row_real = rows_ref[slot, 0, pl.ds(a, 1), :]
            row_imag = rows_ref[slot, 1, pl.ds(a, 1), :]
            table_ref[slot, pl.ds(a * FINE, FINE), :] = (
                row_real * fine_real - row_imag * fine_imag
            ).astype(jnp.bfloat16)
            table_ref[slot, pl.ds(depth + a * FINE, FINE), :] = (
                row_real * fine_imag + row_imag * fine_real
            ).astype(jnp.bfloat16)
        turns = (facet * YB * ((target_origin(target) + step) % (N_IMAGE // YB))) % N_IMAGE
        cosines, sines = cos_sin(turns, -1.0)
        cosines, sines = weight * cosines, weight * sines
        products = jnp.dot(samples_ref[...], table_ref[slot], preferred_element_type=jnp.float32)
        products = products.reshape(window, 2, row_count, columns)
        total_real = jnp.zeros((row_count, columns), jnp.float32)
        total_imag = jnp.zeros((row_count, columns), jnp.float32)
        for number in range(window):
            real_part = products[number, 0]
            imag_part = products[number, 1]
            cosine = cosines[number : number + 1]
            sine = sines[number : number + 1]
            total_real += real_part * cosine - imag_part * sine
            total_imag += real_part * sine + imag_part * cosine
        out_ref[slot, :, :columns] = total_real.astype(jnp.bfloat16)
        out_ref[slot, :, columns:] = total_imag.astype(jnp.bfloat16)


def predict(place, offsets, taper, data):
    columns = taper.shape[1]
    row_count, width = data.shape[2:]
    window = data.shape[0] // 2
    targets = taper.shape[0] // window * offsets.shape[1] // 2
    pair = 8
    coarse = turn_table(np.arange(YB // FINE) * FINE, np.arange(columns))
    fine = turn_table(np.arange(FINE), np.arange(columns))
    whole = pl.BlockSpec(memory_space=pltpu.VMEM)
    scalar = pl.BlockSpec(memory_space=pltpu.SMEM)
    return pl.pallas_call(
        predict_kernel,
        grid=(targets // pair,),
        out_shape=jax.ShapeDtypeStruct((targets, row_count, 2 * columns), jnp.bfloat16),
        in_specs=[scalar, scalar, whole, whole, whole, whole],
        out_specs=pl.BlockSpec((pair, row_count, 2 * columns), lambda i: (i, 0, 0)),
        scratch_shapes=[
            pltpu.VMEM((2, 2 * width // FINE + FINE, 128), jnp.float32),
            pltpu.VMEM((pair, 2, 2 * width // FINE, columns), jnp.float32),
            pltpu.VMEM((pair, 4 * width, columns), jnp.bfloat16),
            pltpu.VMEM((window * 2 * row_count, 4 * width), jnp.bfloat16),
        ],
        compiler_params=pltpu.CompilerParams(vmem_limit_bytes=28 * 1024 * 1024),
    )(place, offsets, taper, coarse, fine, data)


def degrid_kernel(place_ref, own_ref, rim_ref, kernel_ref, out_ref, tiles_ref):
    columns = own_ref.shape[1] // 2
    row_count = own_ref.shape[0]
    blocks, taps = kernel_ref.shape[:2]
    for part in range(2):
        for tile in range(3):
            first = part * columns + tile * 64
            tiles_ref[3 * part + tile, :row_count] = own_ref[:, first : first + 128]
            tiles_ref[3 * part + tile, row_count:] = rim_ref[:, first : first + 128]
    row_at = lax.broadcasted_iota(jnp.int32, (8, 128), 0)
    lane_at = lax.broadcasted_iota(jnp.int32, (8, 128), 1)
    tap_masks = [lane_at // KS == row_at + 8 * half for half in range(2)]
    half_at = lane_at // 64
    tap_at = lane_at % KS

    def group(g, carry):
        parts = []
        for quad in range(2):
            spread = []
            for tile in range(2):
                sums = []
                for part in range(2):
                    merged = jnp.zeros((8, 128), jnp.float32)
                    for half in range(2):
                        b = g * 8 + quad * 4 + tile * 2 + half
                        start = place_ref[blocks + b]
                        cut = (start > 120).astype(jnp.int32) + (start > 184).astype(jnp.int32)
                        patch = tiles_ref[3 * part + cut, pl.ds(place_ref[b], KS), :]
                        picks = tap_at + (start - 64 * cut)
                        patch = jnp.take_along_axis(patch, picks, axis=1, mode="promise_in_bounds")
                        merged = jnp.where(tap_masks[half], patch, merged)
                    sums.append(jnp.sum(merged, axis=0, keepdims=True))
                wanted = half_at + 2 * tile
                value = jnp.where(row_at == wanted, sums[0], 0.0)
                spread.append(jnp.where(row_at == wanted + 4, sums[1], value))
            weights = kernel_ref[pl.ds(g * 8 + quad * 4, 4)].reshape(4 * taps, 128)
            exact = jnp.concatenate(spread, axis=1)
            high = exact.astype(jnp.bfloat16)
            low = (exact - high.astype(jnp.float32)).astype(jnp.bfloat16)
            stacked = jnp.concatenate([high, low], axis=0)
            product = jnp.dot(stacked, weights, preferred_element_type=jnp.float32)
            parts.append(product[:8] + product[8:])
        live = g * 8 + row_at < place_ref[2 * blocks]
        for part in range(2):
            value = jnp.concatenate([p[4 * part : 4 * part + 4] for p in parts], axis=0)
            out_ref[pl.ds(pl.multiple_of(g * 8, 8), 8), part * 128 : (part + 1) * 128] = jnp.where(
                live, value, 0.0
            )
        return carry

    lax.fori_loop(0, kernel_ref.shape[0] // 8, group, 0, unroll=2)


def degrid(places, own, rim, kernel):
    whole = pl.BlockSpec(memory_space=pltpu.VMEM)
    scalar = pl.BlockSpec(memory_space=pltpu.SMEM)
    return pl.pallas_call(
        degrid_kernel,
        out_shape=jax.ShapeDtypeStruct((kernel.shape[0], 2 * kernel.shape[2]), jnp.float32),
        in_specs=[scalar, whole, whole, whole],
        out_specs=whole,
        scratch_shapes=[pltpu.VMEM((6, own.shape[0] + KS, 128), jnp.float32)],
        compiler_params=pltpu.CompilerParams(vmem_limit_bytes=32 * 1024 * 1024),
    )(places, own, rim, kernel)


def cos_sin(turns, sign):
    angles = turns.astype(jnp.float32) * (2.0 * math.pi / N_IMAGE)
    return jnp.cos(angles), sign * jnp.sin(angles)


def on_device(facet_data, facet_taper, subgrid_offsets, kernels, block_row, block_col, block_count):
    facet_index = lax.axis_index("facet")
    sub_index = lax.axis_index("sub")
    facets = lax.axis_size("facet")
    subs = lax.axis_size("sub")
    vis_count = lax.axis_size("vis")
    columns = facet_taper.shape[1]
    row_count = facet_data.shape[2]
    place = jnp.stack([facet_index, sub_index // 2, sub_index % 2])
    places = jnp.concatenate([block_row[0, 0, 0], block_col[0, 0, 0], block_count[0, 0]])
    place, places = lax.optimization_barrier((place, places))
    far_groups = [
        [z * subs + s + core for z in range(first, facets, NEAR) for core in range(2)]
        for first in range(NEAR)
        for s in range(0, subs, 2)
    ]
    near_groups = [
        [(first + dz) % facets * subs + s for dz in range(NEAR) for s in range(core, subs, 2)]
        for core in range(2)
        for first in range(NEAR // 2 * core, facets, NEAR)
    ]
    data = lax.all_gather(facet_data[:, 0], ("facet", "sub"), axis_index_groups=far_groups)
    partial = predict(place, subgrid_offsets, facet_taper, data)
    received = lax.all_to_all(
        partial, ("facet", "sub"), 0, 0, axis_index_groups=near_groups, tiled=True
    )
    summed = jnp.sum(received.astype(jnp.float32), axis=0)
    rim = lax.ppermute(summed[:KS], "vis", [(i, i - 1) for i in range(1, vis_count)])
    visibilities = degrid(places, summed, rim, kernels[0, 0, 0])
    return (
        summed.reshape(1, 1, row_count, 2 * columns),
        visibilities.reshape((1, 1, 1) + visibilities.shape),
    )


def solution(mesh):
    return jax.shard_map(
        on_device,
        mesh=mesh,
        in_specs=(
            P(None, "facet", "vis", "sub"),
            P(),
            P(),
            P("facet", "sub", "vis", None, None, None),
            P("facet", "sub", "vis", None),
            P("facet", "sub", "vis", None),
            P("facet", "sub", "vis"),
        ),
        out_specs=(P("facet", "sub", "vis", None), P("facet", "sub", "vis", None, None)),
        check_vma=False,
    )
```

```python
import math

import jax
import jax.numpy as jnp
import numpy as np
from jax import lax
from jax.experimental import pallas as pl
from jax.experimental.pallas import tpu as pltpu
from jax.sharding import PartitionSpec as P

N_IMAGE = 65536
YB = 2048
KS = 8
FINE = 32
NEAR = 2
TARGETS = 8


def turn_table(left, right):
    turns = (left.astype(np.int64)[:, None] * right.astype(np.int64)[None, :]) % N_IMAGE
    angles = turns * (2.0 * math.pi / N_IMAGE)
    return np.stack([np.cos(angles), -np.sin(angles)]).astype(np.float32)


def predict_kernel(place_ref, offset_ref, taper_ref, coarse_ref, fine_ref, own_ref, mate_ref, out_ref, steps_ref, rows_ref, table_ref, samples_ref):
    columns = coarse_ref.shape[2]
    window, _, row_count, width = own_ref.shape
    targets = out_ref.shape[0]
    facets, subs = offset_ref.shape
    block_rows = width // FINE
    near = facets // window
    z, sub = place_ref[0], place_ref[1]
    core = sub % 2
    z_first = (z + near - core) // near * near + core + facets - near

    def target_origin(target):
        row = (z_first + target // (subs // 2)) % facets
        column = target % (subs // 2) * 2 + core
        return (offset_ref[row, column] + N_IMAGE - columns // 2) % N_IMAGE

    lane = lax.broadcasted_iota(jnp.int32, steps_ref.shape[1:], 1)
    row = lax.broadcasted_iota(jnp.int32, steps_ref.shape[1:], 0)
    origins = jnp.zeros_like(lane)
    for target in range(targets):
        origins = jnp.where(lane == target, target_origin(target), origins)
    own_step = sub * width + row * FINE
    mate_step = (sub + 1 - 2 * core) * width + (row - block_rows) * FINE
    multiples = jnp.where(
        row < block_rows, own_step, jnp.where(row < 2 * block_rows, mate_step, row - 2 * block_rows)
    )
    real_part, imag_part = cos_sin((multiples * origins) % N_IMAGE, -1.0)
    steps_ref[0] = real_part
    steps_ref[1] = imag_part
    for number in range(window):
        for side, ref in enumerate((own_ref, mate_ref)):
            rows = slice(2 * number * row_count, (2 * number + 1) * row_count)
            after = slice((2 * number + 1) * row_count, (2 * number + 2) * row_count)
            left = slice(side * width, (side + 1) * width)
            right = slice((2 + side) * width, (3 + side) * width)
            samples_ref[rows, left] = ref[number, 0]
            samples_ref[rows, right] = -ref[number, 1]
            samples_ref[after, left] = ref[number, 1]
            samples_ref[after, right] = ref[number, 0]

    coarse_parts = []
    for part in range(2):
        sides = [
            coarse_ref[part, pl.ds(pl.multiple_of(side * block_rows, block_rows), block_rows), :]
            for side in (sub, sub + 1 - 2 * core)
        ]
        coarse_parts.append(jnp.concatenate(sides, axis=0))
    coarse_real, coarse_imag = coarse_parts
    tapers = [taper_ref[pl.ds(near * number + z % near, 1), :] for number in range(window)]
    weight = jnp.concatenate(tapers, axis=0) * (1.0 / math.sqrt(YB * facets))
    facet = near * lax.broadcasted_iota(jnp.int32, (window, columns), 0) + z % near
    step = lax.broadcasted_iota(jnp.int32, (window, columns), 1)
    for slot in range(targets):
        real_step = steps_ref[0, :, slot : slot + 1]
        imag_step = steps_ref[1, :, slot : slot + 1]
        far_real, far_imag = real_step[: 2 * block_rows], imag_step[: 2 * block_rows]
        low_real, low_imag = real_step[2 * block_rows :], imag_step[2 * block_rows :]
        rows_ref[slot, 0] = far_real * coarse_real - far_imag * coarse_imag
        rows_ref[slot, 1] = far_real * coarse_imag + far_imag * coarse_real
        fine_real = low_real * fine_ref[0] - low_imag * fine_ref[1]
        fine_imag = low_real * fine_ref[1] + low_imag * fine_ref[0]
        for a in range(2 * block_rows):
            row_real = rows_ref[slot, 0, pl.ds(a, 1), :]
            row_imag = rows_ref[slot, 1, pl.ds(a, 1), :]
            table_ref[slot, pl.ds(a * FINE, FINE), :] = (
                row_real * fine_real - row_imag * fine_imag
            ).astype(jnp.bfloat16)
            table_ref[slot, pl.ds(2 * width + a * FINE, FINE), :] = (
                row_real * fine_imag + row_imag * fine_real
            ).astype(jnp.bfloat16)
        turns = (facet * YB * ((target_origin(slot) + step) % (N_IMAGE // YB))) % N_IMAGE
        cosines, sines = cos_sin(turns, -1.0)
        cosines, sines = weight * cosines, weight * sines
        products = jnp.dot(samples_ref[...], table_ref[slot], preferred_element_type=jnp.float32)
        products = products.reshape(window, 2, row_count, columns)
        total_real = jnp.zeros((row_count, columns), jnp.float32)
        total_imag = jnp.zeros((row_count, columns), jnp.float32)
        for number in range(window):
            real_part = products[number, 0]
            imag_part = products[number, 1]
            cosine = cosines[number : number + 1]
            sine = sines[number : number + 1]
            total_real += real_part * cosine - imag_part * sine
            total_imag += real_part * sine + imag_part * cosine
        out_ref[slot, :, :columns] = total_real.astype(jnp.bfloat16)
        out_ref[slot, :, columns:] = total_imag.astype(jnp.bfloat16)


def predict(place, offsets, taper, own, mate, targets):
    columns = taper.shape[1]
    row_count, width = own.shape[2:]
    coarse = turn_table(np.arange(YB // FINE) * FINE, np.arange(columns))
    fine = turn_table(np.arange(FINE), np.arange(columns))
    whole = pl.BlockSpec(memory_space=pltpu.VMEM)
    scalar = pl.BlockSpec(memory_space=pltpu.SMEM)
    return pl.pallas_call(
        predict_kernel,
        out_shape=jax.ShapeDtypeStruct((targets, row_count, 2 * columns), jnp.bfloat16),
        in_specs=[scalar, scalar, whole, whole, whole, whole, whole],
        out_specs=whole,
        scratch_shapes=[
            pltpu.VMEM((2, 2 * width // FINE + FINE, 128), jnp.float32),
            pltpu.VMEM((targets, 2, 2 * width // FINE, columns), jnp.float32),
            pltpu.VMEM((targets, 4 * width, columns), jnp.bfloat16),
            pltpu.VMEM((own.shape[0] * 2 * row_count, 4 * width), jnp.bfloat16),
        ],
        compiler_params=pltpu.CompilerParams(vmem_limit_bytes=28 * 1024 * 1024),
    )(place, offsets, taper, coarse, fine, own, mate)


def degrid_kernel(place_ref, own_ref, rim_ref, kernel_ref, out_ref, tiles_ref):
    columns = own_ref.shape[1] // 2
    row_count = own_ref.shape[0]
    blocks, taps = kernel_ref.shape[:2]
    for part in range(2):
        for tile in range(3):
            first = part * columns + tile * 64
            tiles_ref[3 * part + tile, :row_count] = own_ref[:, first : first + 128]
            tiles_ref[3 * part + tile, row_count:] = rim_ref[:, first : first + 128]
    row_at = lax.broadcasted_iota(jnp.int32, (8, 128), 0)
    lane_at = lax.broadcasted_iota(jnp.int32, (8, 128), 1)
    tap_masks = [lane_at // KS == row_at + 8 * half for half in range(2)]
    half_at = lane_at // 64
    tap_at = lane_at % KS

    def group(g, carry):
        parts = []
        for quad in range(2):
            spread = []
            for tile in range(2):
                sums = []
                for part in range(2):
                    merged = jnp.zeros((8, 128), jnp.float32)
                    for half in range(2):
                        b = g * 8 + quad * 4 + tile * 2 + half
                        start = place_ref[blocks + b]
                        cut = (start > 120).astype(jnp.int32) + (start > 184).astype(jnp.int32)
                        patch = tiles_ref[3 * part + cut, pl.ds(place_ref[b], KS), :]
                        picks = tap_at + (start - 64 * cut)
                        patch = jnp.take_along_axis(patch, picks, axis=1, mode="promise_in_bounds")
                        merged = jnp.where(tap_masks[half], patch, merged)
                    sums.append(jnp.sum(merged, axis=0, keepdims=True))
                wanted = half_at + 2 * tile
                value = jnp.where(row_at == wanted, sums[0], 0.0)
                spread.append(jnp.where(row_at == wanted + 4, sums[1], value))
            weights = kernel_ref[pl.ds(g * 8 + quad * 4, 4)].reshape(4 * taps, 128)
            exact = jnp.concatenate(spread, axis=1)
            high = exact.astype(jnp.bfloat16)
            low = (exact - high.astype(jnp.float32)).astype(jnp.bfloat16)
            stacked = jnp.concatenate([high, low], axis=0)
            product = jnp.dot(stacked, weights, preferred_element_type=jnp.float32)
            parts.append(product[:8] + product[8:])
        live = g * 8 + row_at < place_ref[2 * blocks]
        for part in range(2):
            value = jnp.concatenate([p[4 * part : 4 * part + 4] for p in parts], axis=0)
            out_ref[pl.ds(pl.multiple_of(g * 8, 8), 8), part * 128 : (part + 1) * 128] = jnp.where(
                live, value, 0.0
            )
        return carry

    lax.fori_loop(0, kernel_ref.shape[0] // 8, group, 0, unroll=8)


def degrid(places, own, rim, kernel):
    whole = pl.BlockSpec(memory_space=pltpu.VMEM)
    scalar = pl.BlockSpec(memory_space=pltpu.SMEM)
    return pl.pallas_call(
        degrid_kernel,
        out_shape=jax.ShapeDtypeStruct((kernel.shape[0], 2 * kernel.shape[2]), jnp.float32),
        in_specs=[scalar, whole, whole, whole],
        out_specs=whole,
        scratch_shapes=[pltpu.VMEM((6, own.shape[0] + KS, 128), jnp.float32)],
        compiler_params=pltpu.CompilerParams(vmem_limit_bytes=32 * 1024 * 1024),
    )(places, own, rim, kernel)


def cos_sin(turns, sign):
    angles = turns.astype(jnp.float32) * (2.0 * math.pi / N_IMAGE)
    return jnp.cos(angles), sign * jnp.sin(angles)


def near_groups(facets, subs):
    groups = []
    for core in range(2):
        for number in range(facets // NEAR):
            group = []
            for dz in range(NEAR):
                z = (NEAR * number + core + dz) % facets
                group.extend(z * subs + s for s in range(core, subs, 2))
            groups.append(group)
    return groups


def on_device(facet_data, facet_taper, subgrid_offsets, kernels, block_row, block_col, block_count):
    facet_index = lax.axis_index("facet")
    sub_index = lax.axis_index("sub")
    facets = lax.axis_size("facet")
    subs = lax.axis_size("sub")
    vis_count = lax.axis_size("vis")
    columns = facet_taper.shape[1]
    row_count = facet_data.shape[2]
    far_groups = [[j + NEAR * k for k in range(facets // NEAR)] for j in range(NEAR)]
    own = lax.all_gather(facet_data[:, 0], "facet", axis_index_groups=far_groups)
    mate = lax.ppermute(own, "sub", [(s, s ^ 1) for s in range(subs)])
    place = jnp.stack([facet_index, sub_index])
    places = jnp.concatenate([block_row[0, 0, 0], block_col[0, 0, 0], block_count[0, 0]])
    place, places = lax.optimization_barrier((place, places))
    partial = predict(place, subgrid_offsets, facet_taper, own, mate, TARGETS)
    received = lax.all_to_all(
        partial, ("facet", "sub"), 0, 0, axis_index_groups=near_groups(facets, subs), tiled=True
    )
    summed = jnp.sum(received.astype(jnp.float32), axis=0)
    rim = lax.ppermute(summed[:KS], "vis", [(i, i - 1) for i in range(1, vis_count)])
    visibilities = degrid(places, summed, rim, kernels[0, 0, 0])
    return (
        summed.reshape(1, 1, row_count, 2 * columns),
        visibilities.reshape((1, 1, 1) + visibilities.shape),
    )


def solution(mesh):
    return jax.shard_map(
        on_device,
        mesh=mesh,
        in_specs=(
            P(None, "facet", "vis", "sub"),
            P(),
            P(),
            P("facet", "sub", "vis", None, None, None),
            P("facet", "sub", "vis", None),
            P("facet", "sub", "vis", None),
            P("facet", "sub", "vis"),
        ),
        out_specs=(P("facet", "sub", "vis", None), P("facet", "sub", "vis", None, None)),
        check_vma=False,
    )
```

```python
import math

import jax
import jax.numpy as jnp
import numpy as np
from jax import lax
from jax.experimental import pallas as pl
from jax.experimental.pallas import tpu as pltpu
from jax.sharding import PartitionSpec as P

N_IMAGE = 65536
YB = 2048
KS = 8
FINE = 32
NEAR = 2
TARGETS = 8


def turn_table(left, right):
    turns = (left.astype(np.int64)[:, None] * right.astype(np.int64)[None, :]) % N_IMAGE
    angles = turns * (2.0 * math.pi / N_IMAGE)
    return np.stack([np.cos(angles), -np.sin(angles)]).astype(np.float32)


def predict_kernel(offset_ref, taper_ref, coarse_ref, fine_ref, own_ref, mate_ref, out_ref, steps_ref, rows_ref, table_ref, samples_ref):
    columns = coarse_ref.shape[2]
    window, _, row_count, width = own_ref.shape
    targets = out_ref.shape[0]
    facets, subs = offset_ref.shape
    block_rows = width // FINE
    near = facets // window
    z, sub = lax.axis_index("facet"), lax.axis_index("sub")
    core = sub % 2
    z_first = (z + near - core) // near * near + core + facets - near

    def target_origin(target):
        row = (z_first + target // (subs // 2)) % facets
        column = target % (subs // 2) * 2 + core
        return (offset_ref[row, column] + N_IMAGE - columns // 2) % N_IMAGE

    lane = lax.broadcasted_iota(jnp.int32, steps_ref.shape[1:], 1)
    row = lax.broadcasted_iota(jnp.int32, steps_ref.shape[1:], 0)
    origins = jnp.zeros_like(lane)
    for target in range(targets):
        origins = jnp.where(lane == target, target_origin(target), origins)
    own_step = sub * width + row * FINE
    mate_step = (sub + 1 - 2 * core) * width + (row - block_rows) * FINE
    multiples = jnp.where(
        row < block_rows, own_step, jnp.where(row < 2 * block_rows, mate_step, row - 2 * block_rows)
    )
    real_part, imag_part = cos_sin((multiples * origins) % N_IMAGE, -1.0)
    steps_ref[0] = real_part
    steps_ref[1] = imag_part
    for number in range(window):
        for side, ref in enumerate((own_ref, mate_ref)):
            rows = slice(2 * number * row_count, (2 * number + 1) * row_count)
            after = slice((2 * number + 1) * row_count, (2 * number + 2) * row_count)
            left = slice(side * width, (side + 1) * width)
            right = slice((2 + side) * width, (3 + side) * width)
            samples_ref[rows, left] = ref[number, 0]
            samples_ref[rows, right] = -ref[number, 1]
            samples_ref[after, left] = ref[number, 1]
            samples_ref[after, right] = ref[number, 0]

    coarse_parts = []
    for part in range(2):
        sides = [
            coarse_ref[part, pl.ds(pl.multiple_of(side * block_rows, block_rows), block_rows), :]
            for side in (sub, sub + 1 - 2 * core)
        ]
        coarse_parts.append(jnp.concatenate(sides, axis=0))
    coarse_real, coarse_imag = coarse_parts
    tapers = [taper_ref[pl.ds(near * number + z % near, 1), :] for number in range(window)]
    weight = jnp.concatenate(tapers, axis=0) * (1.0 / math.sqrt(YB * facets))
    facet = near * lax.broadcasted_iota(jnp.int32, (window, columns), 0) + z % near
    step = lax.broadcasted_iota(jnp.int32, (window, columns), 1)
    for slot in range(targets):
        real_step = steps_ref[0, :, slot : slot + 1]
        imag_step = steps_ref[1, :, slot : slot + 1]
        far_real, far_imag = real_step[: 2 * block_rows], imag_step[: 2 * block_rows]
        low_real, low_imag = real_step[2 * block_rows :], imag_step[2 * block_rows :]
        rows_ref[slot, 0] = far_real * coarse_real - far_imag * coarse_imag
        rows_ref[slot, 1] = far_real * coarse_imag + far_imag * coarse_real
        fine_real = low_real * fine_ref[0] - low_imag * fine_ref[1]
        fine_imag = low_real * fine_ref[1] + low_imag * fine_ref[0]
        for a in range(2 * block_rows):
            row_real = rows_ref[slot, 0, pl.ds(a, 1), :]
            row_imag = rows_ref[slot, 1, pl.ds(a, 1), :]
            table_ref[slot, pl.ds(a * FINE, FINE), :] = (
                row_real * fine_real - row_imag * fine_imag
            ).astype(jnp.bfloat16)
            table_ref[slot, pl.ds(2 * width + a * FINE, FINE), :] = (
                row_real * fine_imag + row_imag * fine_real
            ).astype(jnp.bfloat16)
        turns = (facet * YB * ((target_origin(slot) + step) % (N_IMAGE // YB))) % N_IMAGE
        cosines, sines = cos_sin(turns, -1.0)
        cosines, sines = weight * cosines, weight * sines
        products = jnp.dot(samples_ref[...], table_ref[slot], preferred_element_type=jnp.float32)
        products = products.reshape(window, 2, row_count, columns)
        total_real = jnp.zeros((row_count, columns), jnp.float32)
        total_imag = jnp.zeros((row_count, columns), jnp.float32)
        for number in range(window):
            real_part = products[number, 0]
            imag_part = products[number, 1]
            cosine = cosines[number : number + 1]
            sine = sines[number : number + 1]
            total_real += real_part * cosine - imag_part * sine
            total_imag += real_part * sine + imag_part * cosine
        out_ref[slot, :, :columns] = total_real.astype(jnp.bfloat16)
        out_ref[slot, :, columns:] = total_imag.astype(jnp.bfloat16)


def predict(offsets, taper, own, mate, targets):
    columns = taper.shape[1]
    row_count, width = own.shape[2:]
    coarse = turn_table(np.arange(YB // FINE) * FINE, np.arange(columns))
    fine = turn_table(np.arange(FINE), np.arange(columns))
    whole = pl.BlockSpec(memory_space=pltpu.VMEM)
    scalar = pl.BlockSpec(memory_space=pltpu.SMEM)
    return pl.pallas_call(
        predict_kernel,
        out_shape=jax.ShapeDtypeStruct((targets, row_count, 2 * columns), jnp.bfloat16),
        in_specs=[scalar, whole, whole, whole, whole, whole],
        out_specs=whole,
        scratch_shapes=[
            pltpu.VMEM((2, 2 * width // FINE + FINE, 128), jnp.float32),
            pltpu.VMEM((targets, 2, 2 * width // FINE, columns), jnp.float32),
            pltpu.VMEM((targets, 4 * width, columns), jnp.bfloat16),
            pltpu.VMEM((own.shape[0] * 2 * row_count, 4 * width), jnp.bfloat16),
        ],
        compiler_params=pltpu.CompilerParams(vmem_limit_bytes=28 * 1024 * 1024),
    )(offsets, taper, coarse, fine, own, mate)


def degrid_kernel(place_ref, own_ref, rim_ref, kernel_ref, out_ref, tiles_ref):
    columns = own_ref.shape[1] // 2
    row_count = own_ref.shape[0]
    blocks, taps = kernel_ref.shape[:2]
    for part in range(2):
        for tile in range(3):
            first = part * columns + tile * 64
            tiles_ref[3 * part + tile, :row_count] = own_ref[:, first : first + 128]
            tiles_ref[3 * part + tile, row_count:] = rim_ref[:, first : first + 128]
    row_at = lax.broadcasted_iota(jnp.int32, (8, 128), 0)
    lane_at = lax.broadcasted_iota(jnp.int32, (8, 128), 1)
    tap_masks = [lane_at // KS == row_at + 8 * half for half in range(2)]
    half_at = lane_at // 64
    tap_at = lane_at % KS

    def group(g, carry):
        parts = []
        for quad in range(2):
            spread = []
            for tile in range(2):
                sums = []
                for part in range(2):
                    merged = jnp.zeros((8, 128), jnp.float32)
                    for half in range(2):
                        b = g * 8 + quad * 4 + tile * 2 + half
                        start = place_ref[blocks + b]
                        cut = (start > 120).astype(jnp.int32) + (start > 184).astype(jnp.int32)
                        patch = tiles_ref[3 * part + cut, pl.ds(place_ref[b], KS), :]
                        picks = tap_at + (start - 64 * cut)
                        patch = jnp.take_along_axis(patch, picks, axis=1, mode="promise_in_bounds")
                        merged = jnp.where(tap_masks[half], patch, merged)
                    sums.append(jnp.sum(merged, axis=0, keepdims=True))
                wanted = half_at + 2 * tile
                value = jnp.where(row_at == wanted, sums[0], 0.0)
                spread.append(jnp.where(row_at == wanted + 4, sums[1], value))
            weights = kernel_ref[pl.ds(g * 8 + quad * 4, 4)].reshape(4 * taps, 128)
            exact = jnp.concatenate(spread, axis=1)
            high = exact.astype(jnp.bfloat16)
            low = (exact - high.astype(jnp.float32)).astype(jnp.bfloat16)
            stacked = jnp.concatenate([high, low], axis=0)
            product = jnp.dot(stacked, weights, preferred_element_type=jnp.float32)
            parts.append(product[:8] + product[8:])
        live = g * 8 + row_at < place_ref[2 * blocks]
        for part in range(2):
            value = jnp.concatenate([p[4 * part : 4 * part + 4] for p in parts], axis=0)
            out_ref[pl.ds(pl.multiple_of(g * 8, 8), 8), part * 128 : (part + 1) * 128] = jnp.where(
                live, value, 0.0
            )
        return carry

    lax.fori_loop(0, kernel_ref.shape[0] // 8, group, 0, unroll=8)


def degrid(places, own, rim, kernel):
    whole = pl.BlockSpec(memory_space=pltpu.VMEM)
    scalar = pl.BlockSpec(memory_space=pltpu.SMEM)
    return pl.pallas_call(
        degrid_kernel,
        out_shape=jax.ShapeDtypeStruct((kernel.shape[0], 2 * kernel.shape[2]), jnp.float32),
        in_specs=[scalar, whole, whole, whole],
        out_specs=whole,
        scratch_shapes=[pltpu.VMEM((6, own.shape[0] + KS, 128), jnp.float32)],
        compiler_params=pltpu.CompilerParams(vmem_limit_bytes=32 * 1024 * 1024),
    )(places, own, rim, kernel)


def cos_sin(turns, sign):
    angles = turns.astype(jnp.float32) * (2.0 * math.pi / N_IMAGE)
    return jnp.cos(angles), sign * jnp.sin(angles)


def near_groups(facets, subs):
    groups = []
    for core in range(2):
        for number in range(facets // NEAR):
            group = []
            for dz in range(NEAR):
                z = (NEAR * number + core + dz) % facets
                group.extend(z * subs + s for s in range(core, subs, 2))
            groups.append(group)
    return groups


def on_device(facet_data, facet_taper, subgrid_offsets, kernels, block_row, block_col, block_count):
    facets = lax.axis_size("facet")
    subs = lax.axis_size("sub")
    vis_count = lax.axis_size("vis")
    columns = facet_taper.shape[1]
    row_count = facet_data.shape[2]
    far_groups = [[j + NEAR * k for k in range(facets // NEAR)] for j in range(NEAR)]
    own = lax.all_gather(facet_data[:, 0], "facet", axis_index_groups=far_groups)
    mate = lax.ppermute(own, "sub", [(s, s ^ 1) for s in range(subs)])
    places = jnp.concatenate([block_row[0, 0, 0], block_col[0, 0, 0], block_count[0, 0]])
    offsets, places = lax.optimization_barrier((subgrid_offsets, places))
    partial = predict(offsets, facet_taper, own, mate, TARGETS)
    received = lax.all_to_all(
        partial, ("facet", "sub"), 0, 0, axis_index_groups=near_groups(facets, subs), tiled=True
    )
    summed = jnp.sum(received.astype(jnp.float32), axis=0)
    rim = lax.ppermute(summed[:KS], "vis", [(i, i - 1) for i in range(1, vis_count)])
    visibilities = degrid(places, summed, rim, kernels[0, 0, 0])
    return (
        summed.reshape(1, 1, row_count, 2 * columns),
        visibilities.reshape((1, 1, 1) + visibilities.shape),
    )


def solution(mesh):
    return jax.shard_map(
        on_device,
        mesh=mesh,
        in_specs=(
            P(None, "facet", "vis", "sub"),
            P(),
            P(),
            P("facet", "sub", "vis", None, None, None),
            P("facet", "sub", "vis", None),
            P("facet", "sub", "vis", None),
            P("facet", "sub", "vis"),
        ),
        out_specs=(P("facet", "sub", "vis", None), P("facet", "sub", "vis", None, None)),
        check_vma=False,
    )
```

```python
import math

import jax
import jax.numpy as jnp
import numpy as np
from jax import lax
from jax.experimental import pallas as pl
from jax.experimental.pallas import tpu as pltpu
from jax.sharding import PartitionSpec as P

N_IMAGE = 65536
YB = 2048
KS = 8
FINE = 32
NEAR = 2
TARGETS = 8


def turn_table(left, right):
    turns = (left.astype(np.int64)[:, None] * right.astype(np.int64)[None, :]) % N_IMAGE
    angles = turns * (2.0 * math.pi / N_IMAGE)
    return np.stack([np.cos(angles), -np.sin(angles)]).astype(np.float32)


def predict_kernel(offset_ref, taper_ref, coarse_ref, fine_ref, own_ref, mate_ref, out_ref, steps_ref, rows_ref, table_ref, samples_ref):
    columns = coarse_ref.shape[2]
    window, _, row_count, width = own_ref.shape
    targets = out_ref.shape[0]
    facets, subs = offset_ref.shape
    block_rows = width // FINE
    near = facets // window
    z, sub = lax.axis_index("facet"), lax.axis_index("sub")
    core = sub % 2
    z_first = (z + near - core) // near * near + core + facets - near

    def target_origin(target):
        row = (z_first + target // (subs // 2)) % facets
        column = target % (subs // 2) * 2 + core
        return (offset_ref[row, column] + N_IMAGE - columns // 2) % N_IMAGE

    lane = lax.broadcasted_iota(jnp.int32, steps_ref.shape[1:], 1)
    row = lax.broadcasted_iota(jnp.int32, steps_ref.shape[1:], 0)
    origins = jnp.zeros_like(lane)
    for target in range(targets):
        origins = jnp.where(lane == target, target_origin(target), origins)
    own_step = sub * width + row * FINE
    mate_step = (sub + 1 - 2 * core) * width + (row - block_rows) * FINE
    multiples = jnp.where(
        row < block_rows, own_step, jnp.where(row < 2 * block_rows, mate_step, row - 2 * block_rows)
    )
    real_part, imag_part = cos_sin((multiples * origins) % N_IMAGE, -1.0)
    steps_ref[0] = real_part
    steps_ref[1] = imag_part
    for number in range(window):
        for side, ref in enumerate((own_ref, mate_ref)):
            rows = slice(2 * number * row_count, (2 * number + 1) * row_count)
            after = slice((2 * number + 1) * row_count, (2 * number + 2) * row_count)
            left = slice(side * width, (side + 1) * width)
            right = slice((2 + side) * width, (3 + side) * width)
            samples_ref[rows, left] = ref[number, 0]
            samples_ref[rows, right] = -ref[number, 1]
            samples_ref[after, left] = ref[number, 1]
            samples_ref[after, right] = ref[number, 0]

    coarse_parts = []
    for part in range(2):
        sides = [
            coarse_ref[part, pl.ds(pl.multiple_of(side * block_rows, block_rows), block_rows), :]
            for side in (sub, sub + 1 - 2 * core)
        ]
        coarse_parts.append(jnp.concatenate(sides, axis=0))
    coarse_real, coarse_imag = coarse_parts
    tapers = [taper_ref[pl.ds(near * number + z % near, 1), :] for number in range(window)]
    weight = jnp.concatenate(tapers, axis=0) * (1.0 / math.sqrt(YB * facets))
    facet = near * lax.broadcasted_iota(jnp.int32, (window, columns), 0) + z % near
    step = lax.broadcasted_iota(jnp.int32, (window, columns), 1)
    for slot in range(targets):
        real_step = steps_ref[0, :, slot : slot + 1]
        imag_step = steps_ref[1, :, slot : slot + 1]
        far_real, far_imag = real_step[: 2 * block_rows], imag_step[: 2 * block_rows]
        low_real, low_imag = real_step[2 * block_rows :], imag_step[2 * block_rows :]
        rows_ref[slot, 0] = far_real * coarse_real - far_imag * coarse_imag
        rows_ref[slot, 1] = far_real * coarse_imag + far_imag * coarse_real
        fine_real = low_real * fine_ref[0] - low_imag * fine_ref[1]
        fine_imag = low_real * fine_ref[1] + low_imag * fine_ref[0]
        for a in range(2 * block_rows):
            row_real = rows_ref[slot, 0, pl.ds(a, 1), :]
            row_imag = rows_ref[slot, 1, pl.ds(a, 1), :]
            table_ref[slot, pl.ds(a * FINE, FINE), :] = (
                row_real * fine_real - row_imag * fine_imag
            ).astype(jnp.bfloat16)
            table_ref[slot, pl.ds(2 * width + a * FINE, FINE), :] = (
                row_real * fine_imag + row_imag * fine_real
            ).astype(jnp.bfloat16)
        turns = (facet * YB * ((target_origin(slot) + step) % (N_IMAGE // YB))) % N_IMAGE
        cosines, sines = cos_sin(turns, -1.0)
        cosines, sines = weight * cosines, weight * sines
        products = jnp.dot(samples_ref[...], table_ref[slot], preferred_element_type=jnp.float32)
        products = products.reshape(window, 2, row_count, columns)
        total_real = jnp.zeros((row_count, columns), jnp.float32)
        total_imag = jnp.zeros((row_count, columns), jnp.float32)
        for number in range(window):
            real_part = products[number, 0]
            imag_part = products[number, 1]
            cosine = cosines[number : number + 1]
            sine = sines[number : number + 1]
            total_real += real_part * cosine - imag_part * sine
            total_imag += real_part * sine + imag_part * cosine
        out_ref[slot, :, :columns] = total_real.astype(jnp.bfloat16)
        out_ref[slot, :, columns:] = total_imag.astype(jnp.bfloat16)


def predict(offsets, taper, own, mate, targets):
    columns = taper.shape[1]
    row_count, width = own.shape[2:]
    coarse = turn_table(np.arange(YB // FINE) * FINE, np.arange(columns))
    fine = turn_table(np.arange(FINE), np.arange(columns))
    whole = pl.BlockSpec(memory_space=pltpu.VMEM)
    scalar = pl.BlockSpec(memory_space=pltpu.SMEM)
    return pl.pallas_call(
        predict_kernel,
        out_shape=jax.ShapeDtypeStruct((targets, row_count, 2 * columns), jnp.bfloat16),
        in_specs=[scalar, whole, whole, whole, whole, whole],
        out_specs=whole,
        scratch_shapes=[
            pltpu.VMEM((2, 2 * width // FINE + FINE, 128), jnp.float32),
            pltpu.VMEM((targets, 2, 2 * width // FINE, columns), jnp.float32),
            pltpu.VMEM((targets, 4 * width, columns), jnp.bfloat16),
            pltpu.VMEM((own.shape[0] * 2 * row_count, 4 * width), jnp.bfloat16),
        ],
        compiler_params=pltpu.CompilerParams(vmem_limit_bytes=28 * 1024 * 1024),
    )(offsets, taper, coarse, fine, own, mate)


def degrid_kernel(place_ref, own_ref, rim_ref, kernel_ref, out_ref, tiles_ref):
    columns = own_ref.shape[1] // 2
    row_count = own_ref.shape[0]
    blocks, taps = kernel_ref.shape[:2]
    for part in range(2):
        for tile in range(3):
            first = part * columns + tile * 64
            tiles_ref[3 * part + tile, :row_count] = own_ref[:, first : first + 128]
            tiles_ref[3 * part + tile, row_count:] = rim_ref[:, first : first + 128]
    row_at = lax.broadcasted_iota(jnp.int32, (8, 128), 0)
    lane_at = lax.broadcasted_iota(jnp.int32, (8, 128), 1)
    tap_masks = [lane_at // KS == row_at + 8 * half for half in range(2)]
    half_at = lane_at // 64
    tap_at = lane_at % KS

    def group(g, carry):
        parts = []
        for quad in range(2):
            spread = []
            for tile in range(2):
                sums = []
                for part in range(2):
                    merged = jnp.zeros((8, 128), jnp.float32)
                    for half in range(2):
                        b = g * 8 + quad * 4 + tile * 2 + half
                        start = place_ref[blocks + b]
                        cut = (start > 120).astype(jnp.int32) + (start > 184).astype(jnp.int32)
                        patch = tiles_ref[3 * part + cut, pl.ds(place_ref[b], KS), :]
                        picks = tap_at + (start - 64 * cut)
                        patch = jnp.take_along_axis(patch, picks, axis=1, mode="promise_in_bounds")
                        merged = jnp.where(tap_masks[half], patch, merged)
                    sums.append(jnp.sum(merged, axis=0, keepdims=True))
                wanted = half_at + 2 * tile
                value = jnp.where(row_at == wanted, sums[0], 0.0)
                spread.append(jnp.where(row_at == wanted + 4, sums[1], value))
            weights = kernel_ref[pl.ds(g * 8 + quad * 4, 4)].reshape(4 * taps, 128)
            exact = jnp.concatenate(spread, axis=1)
            high = exact.astype(jnp.bfloat16)
            low = (exact - high.astype(jnp.float32)).astype(jnp.bfloat16)
            stacked = jnp.concatenate([high, low], axis=0)
            product = jnp.dot(stacked, weights, preferred_element_type=jnp.float32)
            parts.append(product[:8] + product[8:])
        live = g * 8 + row_at < place_ref[2 * blocks]
        for part in range(2):
            value = jnp.concatenate([p[4 * part : 4 * part + 4] for p in parts], axis=0)
            out_ref[pl.ds(pl.multiple_of(g * 8, 8), 8), part * 128 : (part + 1) * 128] = jnp.where(
                live, value, 0.0
            )
        return carry

    lax.fori_loop(0, kernel_ref.shape[0] // 8, group, 0, unroll=8)


def degrid(places, own, rim, kernel):
    whole = pl.BlockSpec(memory_space=pltpu.VMEM)
    scalar = pl.BlockSpec(memory_space=pltpu.SMEM)
    return pl.pallas_call(
        degrid_kernel,
        out_shape=jax.ShapeDtypeStruct((kernel.shape[0], 2 * kernel.shape[2]), jnp.float32),
        in_specs=[scalar, whole, whole, whole],
        out_specs=whole,
        scratch_shapes=[pltpu.VMEM((6, own.shape[0] + KS, 128), jnp.float32)],
        compiler_params=pltpu.CompilerParams(vmem_limit_bytes=32 * 1024 * 1024),
    )(places, own, rim, kernel)


def cos_sin(turns, sign):
    angles = turns.astype(jnp.float32) * (2.0 * math.pi / N_IMAGE)
    return jnp.cos(angles), sign * jnp.sin(angles)


def near_groups(facets, subs):
    groups = []
    for core in range(2):
        for number in range(facets // NEAR):
            group = []
            for dz in range(NEAR):
                z = (NEAR * number + core + dz) % facets
                group.extend(z * subs + s for s in range(core, subs, 2))
            groups.append(group)
    return groups


def on_device(facet_data, facet_taper, subgrid_offsets, kernels, block_row, block_col, block_count):
    facets = lax.axis_size("facet")
    subs = lax.axis_size("sub")
    vis_count = lax.axis_size("vis")
    columns = facet_taper.shape[1]
    row_count = facet_data.shape[2]
    far_groups = [[j + NEAR * k for k in range(facets // NEAR)] for j in range(NEAR)]
    own = lax.all_gather(facet_data[:, 0], "facet", axis_index_groups=far_groups)
    mate = lax.ppermute(own, "sub", [(s, s ^ 1) for s in range(subs)])
    partial = predict(subgrid_offsets, facet_taper, own, mate, TARGETS)
    received = lax.all_to_all(
        partial, ("facet", "sub"), 0, 0, axis_index_groups=near_groups(facets, subs), tiled=True
    )
    summed = jnp.sum(received.astype(jnp.float32), axis=0)
    summed, rows, cols, count = lax.optimization_barrier((summed, block_row, block_col, block_count))
    places = jnp.concatenate([rows[0, 0, 0], cols[0, 0, 0], count[0, 0]])
    rim = lax.ppermute(summed[:KS], "vis", [(i, i - 1) for i in range(1, vis_count)])
    visibilities = degrid(places, summed, rim, kernels[0, 0, 0])
    return (
        summed.reshape(1, 1, row_count, 2 * columns),
        visibilities.reshape((1, 1, 1) + visibilities.shape),
    )


def solution(mesh):
    return jax.shard_map(
        on_device,
        mesh=mesh,
        in_specs=(
            P(None, "facet", "vis", "sub"),
            P(),
            P(),
            P("facet", "sub", "vis", None, None, None),
            P("facet", "sub", "vis", None),
            P("facet", "sub", "vis", None),
            P("facet", "sub", "vis"),
        ),
        out_specs=(P("facet", "sub", "vis", None), P("facet", "sub", "vis", None, None)),
        check_vma=False,
    )
```

```python
import math

import jax
import jax.numpy as jnp
import numpy as np
from jax import lax
from jax.experimental import pallas as pl
from jax.experimental.pallas import tpu as pltpu
from jax.sharding import PartitionSpec as P

N_IMAGE = 65536
YB = 2048
KS = 8
FINE = 32
NEAR = 2
TARGETS = 8


def turn_table(left, right):
    turns = (left.astype(np.int64)[:, None] * right.astype(np.int64)[None, :]) % N_IMAGE
    angles = turns * (2.0 * math.pi / N_IMAGE)
    return np.stack([np.cos(angles), -np.sin(angles)]).astype(np.float32)


def predict_kernel(place_ref, offset_ref, taper_ref, coarse_ref, fine_ref, own_ref, mate_ref, out_ref, steps_ref, rows_ref, table_ref, samples_ref):
    columns = coarse_ref.shape[2]
    window, _, row_count, width = own_ref.shape
    targets = out_ref.shape[0]
    facets, subs = offset_ref.shape
    block_rows = width // FINE
    near = facets // window
    z, sub = place_ref[0], place_ref[1]
    core = sub % 2
    z_first = z // near * near

    def target_origin(target):
        row = z_first + target // (subs // 2)
        column = target % (subs // 2) * 2 + core
        return (offset_ref[row, column] + N_IMAGE - columns // 2) % N_IMAGE

    lane = lax.broadcasted_iota(jnp.int32, steps_ref.shape[1:], 1)
    row = lax.broadcasted_iota(jnp.int32, steps_ref.shape[1:], 0)
    origins = jnp.zeros_like(lane)
    for target in range(targets):
        origins = jnp.where(lane == target, target_origin(target), origins)
    own_step = sub * width + row * FINE
    mate_step = (sub + 1 - 2 * core) * width + (row - block_rows) * FINE
    multiples = jnp.where(
        row < block_rows, own_step, jnp.where(row < 2 * block_rows, mate_step, row - 2 * block_rows)
    )
    real_part, imag_part = cos_sin((multiples * origins) % N_IMAGE, -1.0)
    steps_ref[0] = real_part
    steps_ref[1] = imag_part
    for number in range(window):
        for side, ref in enumerate((own_ref, mate_ref)):
            rows = slice(2 * number * row_count, (2 * number + 1) * row_count)
            after = slice((2 * number + 1) * row_count, (2 * number + 2) * row_count)
            left = slice(side * width, (side + 1) * width)
            right = slice((2 + side) * width, (3 + side) * width)
            samples_ref[rows, left] = ref[number, 0]
            samples_ref[rows, right] = -ref[number, 1]
            samples_ref[after, left] = ref[number, 1]
            samples_ref[after, right] = ref[number, 0]

    coarse_parts = []
    for part in range(2):
        sides = [
            coarse_ref[part, pl.ds(pl.multiple_of(side * block_rows, block_rows), block_rows), :]
            for side in (sub, sub + 1 - 2 * core)
        ]
        coarse_parts.append(jnp.concatenate(sides, axis=0))
    coarse_real, coarse_imag = coarse_parts
    tapers = [taper_ref[pl.ds(near * number + z % near, 1), :] for number in range(window)]
    weight = jnp.concatenate(tapers, axis=0) * (1.0 / math.sqrt(YB * facets))
    facet = near * lax.broadcasted_iota(jnp.int32, (window, columns), 0) + z % near
    step = lax.broadcasted_iota(jnp.int32, (window, columns), 1)
    for slot in range(targets):
        real_step = steps_ref[0, :, slot : slot + 1]
        imag_step = steps_ref[1, :, slot : slot + 1]
        far_real, far_imag = real_step[: 2 * block_rows], imag_step[: 2 * block_rows]
        low_real, low_imag = real_step[2 * block_rows :], imag_step[2 * block_rows :]
        rows_ref[slot, 0] = far_real * coarse_real - far_imag * coarse_imag
        rows_ref[slot, 1] = far_real * coarse_imag + far_imag * coarse_real
        fine_real = low_real * fine_ref[0] - low_imag * fine_ref[1]
        fine_imag = low_real * fine_ref[1] + low_imag * fine_ref[0]
        for a in range(2 * block_rows):
            row_real = rows_ref[slot, 0, pl.ds(a, 1), :]
            row_imag = rows_ref[slot, 1, pl.ds(a, 1), :]
            table_ref[slot, pl.ds(a * FINE, FINE), :] = (
                row_real * fine_real - row_imag * fine_imag
            ).astype(jnp.bfloat16)
            table_ref[slot, pl.ds(2 * width + a * FINE, FINE), :] = (
                row_real * fine_imag + row_imag * fine_real
            ).astype(jnp.bfloat16)
        turns = (facet * YB * ((target_origin(slot) + step) % (N_IMAGE // YB))) % N_IMAGE
        cosines, sines = cos_sin(turns, -1.0)
        cosines, sines = weight * cosines, weight * sines
        products = jnp.dot(samples_ref[...], table_ref[slot], preferred_element_type=jnp.float32)
        products = products.reshape(window, 2, row_count, columns)
        total_real = jnp.zeros((row_count, columns), jnp.float32)
        total_imag = jnp.zeros((row_count, columns), jnp.float32)
        for number in range(window):
            real_part = products[number, 0]
            imag_part = products[number, 1]
            cosine = cosines[number : number + 1]
            sine = sines[number : number + 1]
            total_real += real_part * cosine - imag_part * sine
            total_imag += real_part * sine + imag_part * cosine
        out_ref[slot, :, :columns] = total_real.astype(jnp.bfloat16)
        out_ref[slot, :, columns:] = total_imag.astype(jnp.bfloat16)


def predict(place, offsets, taper, own, mate, targets):
    columns = taper.shape[1]
    row_count, width = own.shape[2:]
    coarse = turn_table(np.arange(YB // FINE) * FINE, np.arange(columns))
    fine = turn_table(np.arange(FINE), np.arange(columns))
    whole = pl.BlockSpec(memory_space=pltpu.VMEM)
    scalar = pl.BlockSpec(memory_space=pltpu.SMEM)
    return pl.pallas_call(
        predict_kernel,
        out_shape=jax.ShapeDtypeStruct((targets, row_count, 2 * columns), jnp.bfloat16),
        in_specs=[scalar, scalar, whole, whole, whole, whole, whole],
        out_specs=whole,
        scratch_shapes=[
            pltpu.VMEM((2, 2 * width // FINE + FINE, 128), jnp.float32),
            pltpu.VMEM((targets, 2, 2 * width // FINE, columns), jnp.float32),
            pltpu.VMEM((targets, 4 * width, columns), jnp.bfloat16),
            pltpu.VMEM((own.shape[0] * 2 * row_count, 4 * width), jnp.bfloat16),
        ],
        compiler_params=pltpu.CompilerParams(vmem_limit_bytes=28 * 1024 * 1024),
    )(place, offsets, taper, coarse, fine, own, mate)


def degrid_kernel(place_ref, own_ref, rim_ref, kernel_ref, out_ref, tiles_ref):
    columns = own_ref.shape[1] // 2
    row_count = own_ref.shape[0]
    blocks, taps = kernel_ref.shape[:2]
    for part in range(2):
        for tile in range(3):
            first = part * columns + tile * 64
            tiles_ref[3 * part + tile, :row_count] = own_ref[:, first : first + 128]
            tiles_ref[3 * part + tile, row_count:] = rim_ref[:, first : first + 128]
    row_at = lax.broadcasted_iota(jnp.int32, (8, 128), 0)
    lane_at = lax.broadcasted_iota(jnp.int32, (8, 128), 1)
    tap_masks = [lane_at // KS == row_at + 8 * half for half in range(2)]
    half_at = lane_at // 64
    tap_at = lane_at % KS

    def group(g, carry):
        parts = []
        for quad in range(2):
            spread = []
            for tile in range(2):
                sums = []
                for part in range(2):
                    merged = jnp.zeros((8, 128), jnp.float32)
                    for half in range(2):
                        b = g * 8 + quad * 4 + tile * 2 + half
                        start = place_ref[blocks + b]
                        cut = (start > 120).astype(jnp.int32) + (start > 184).astype(jnp.int32)
                        patch = tiles_ref[3 * part + cut, pl.ds(place_ref[b], KS), :]
                        picks = tap_at + (start - 64 * cut)
                        patch = jnp.take_along_axis(patch, picks, axis=1, mode="promise_in_bounds")
                        merged = jnp.where(tap_masks[half], patch, merged)
                    sums.append(jnp.sum(merged, axis=0, keepdims=True))
                wanted = half_at + 2 * tile
                value = jnp.where(row_at == wanted, sums[0], 0.0)
                spread.append(jnp.where(row_at == wanted + 4, sums[1], value))
            weights = kernel_ref[pl.ds(g * 8 + quad * 4, 4)].reshape(4 * taps, 128)
            exact = jnp.concatenate(spread, axis=1)
            high = exact.astype(jnp.bfloat16)
            low = (exact - high.astype(jnp.float32)).astype(jnp.bfloat16)
            stacked = jnp.concatenate([high, low], axis=0)
            product = jnp.dot(stacked, weights, preferred_element_type=jnp.float32)
            parts.append(product[:8] + product[8:])
        live = g * 8 + row_at < place_ref[2 * blocks]
        for part in range(2):
            value = jnp.concatenate([p[4 * part : 4 * part + 4] for p in parts], axis=0)
            out_ref[pl.ds(pl.multiple_of(g * 8, 8), 8), part * 128 : (part + 1) * 128] = jnp.where(
                live, value, 0.0
            )
        return carry

    lax.fori_loop(0, kernel_ref.shape[0] // 8, group, 0, unroll=8)


def degrid(places, own, rim, kernel):
    whole = pl.BlockSpec(memory_space=pltpu.VMEM)
    scalar = pl.BlockSpec(memory_space=pltpu.SMEM)
    return pl.pallas_call(
        degrid_kernel,
        out_shape=jax.ShapeDtypeStruct((kernel.shape[0], 2 * kernel.shape[2]), jnp.float32),
        in_specs=[scalar, whole, whole, whole],
        out_specs=whole,
        scratch_shapes=[pltpu.VMEM((6, own.shape[0] + KS, 128), jnp.float32)],
        compiler_params=pltpu.CompilerParams(vmem_limit_bytes=32 * 1024 * 1024),
    )(places, own, rim, kernel)


def cos_sin(turns, sign):
    angles = turns.astype(jnp.float32) * (2.0 * math.pi / N_IMAGE)
    return jnp.cos(angles), sign * jnp.sin(angles)


def near_groups(facets, subs):
    groups = []
    for core in range(2):
        for number in range(facets // NEAR):
            group = []
            for dz in range(NEAR):
                z = NEAR * number + dz
                group.extend(z * subs + s for s in range(core, subs, 2))
            groups.append(group)
    return groups


def on_device(facet_data, facet_taper, subgrid_offsets, kernels, block_row, block_col, block_count):
    facet_index = lax.axis_index("facet")
    sub_index = lax.axis_index("sub")
    facets = lax.axis_size("facet")
    subs = lax.axis_size("sub")
    vis_count = lax.axis_size("vis")
    columns = facet_taper.shape[1]
    row_count = facet_data.shape[2]
    far_groups = [[j + NEAR * k for k in range(facets // NEAR)] for j in range(NEAR)]
    own = lax.all_gather(facet_data[:, 0], "facet", axis_index_groups=far_groups)
    mate = lax.ppermute(own, "sub", [(s, s ^ 1) for s in range(subs)])
    place = jnp.stack([facet_index, sub_index])
    places = jnp.concatenate([block_row[0, 0, 0], block_col[0, 0, 0], block_count[0, 0]])
    place, places = lax.optimization_barrier((place, places))
    partial = predict(place, subgrid_offsets, facet_taper, own, mate, TARGETS)
    received = lax.all_to_all(
        partial, ("facet", "sub"), 0, 0, axis_index_groups=near_groups(facets, subs), tiled=True
    )
    summed = jnp.sum(received.astype(jnp.float32), axis=0)
    rim = lax.ppermute(summed[:KS], "vis", [(i, i - 1) for i in range(1, vis_count)])
    visibilities = degrid(places, summed, rim, kernels[0, 0, 0])
    return (
        summed.reshape(1, 1, row_count, 2 * columns),
        visibilities.reshape((1, 1, 1) + visibilities.shape),
    )


def solution(mesh):
    return jax.shard_map(
        on_device,
        mesh=mesh,
        in_specs=(
            P(None, "facet", "vis", "sub"),
            P(),
            P(),
            P("facet", "sub", "vis", None, None, None),
            P("facet", "sub", "vis", None),
            P("facet", "sub", "vis", None),
            P("facet", "sub", "vis"),
        ),
        out_specs=(P("facet", "sub", "vis", None), P("facet", "sub", "vis", None, None)),
        check_vma=False,
    )
```
